256 devices in a mesh: au: 8 (over y, core), vert: 16 (over x_lo, z), ch: 2 (over x_hi).
Axes of the slice: x: 4 (x_hi: 2, x_lo: 2; x = x_hi * 2 + x_lo), y: 4, z: 8, core: 2. Of those that a mesh axis runs over, the one named last changes fastest.
Arguments:
- visibilities: bfloat16 [131072, 256], P(('au', 'vert'), 'ch'), may hold values from -6 to 6
- owner_tile: int32 [131072, 1], P(('au', 'vert')), may hold values from 0 to 127; in each aligned block of 1024 rows (0 to 1023, 1024 to 2047, ...) at most 32 rows name the same one
- cell_row: int32 [131072], P(('au', 'vert')), may hold values from 0 to 31
- cell_col: int32 [131072], P(('au', 'vert')), may hold values from 0 to 127
- subcell: int32 [2, 131072], P(None, ('au', 'vert')), may hold values from 0 to 7
- channel_weight: float32 [128], P('ch'), may hold values from 0.2 to 1
Outputs:
- grid: float32 [256, 2048, 256], P('au', 'vert', 'ch')
- continuum: float32 [2, 256, 2048], P('ch', 'au', 'vert')
The draws below stay inside these ranges and needn't reach their ends.
Inputs may be any that keep to these rules, and one draw needn't show every extreme that they name: `owner_tile`: among the rows of one device (aligned blocks of 1024 rows), no tile is named by more than 32 rows, a bound that some block reaches.
All inputs are finite; a program needn't handle non-finite values.
Results may differ from the reference program's by a relative error of at most 0.0025.
Values may be sent and summed in bfloat16 or wider, within the bound.
A program may use at most 64 MiB of HBM per device.

```python
import math
import jax
import jax.numpy as jnp
import numpy as np
from jax import lax

CHAN = 128
SUPPORT = 8
OVS = 8
TU = 32
TV = 128
ROWS_DEV = 1024
CAP = 32
ROWS = 131072
NU = 256
NV = 2048
N_AU = 8
N_VERT = 16


def with_ends(values, stream_key, smallest, top_value):
    longest = values.shape.index(max(values.shape))
    spots = []
    for shift in (0, 1):
        where = [jax.random.randint(jax.random.fold_in(stream_key, axis), (), 0, length) for axis, length in enumerate(values.shape)]
        where[longest] = (where[longest] + shift) % values.shape[longest]
        spots.append(tuple(where))
    return values.at[spots[0]].set(smallest).at[spots[1]].set(top_value)


def shard_levels(own_key, extent, cuts, low, largest):
    def one(axis_at, shards_of):
        heights = jax.random.uniform(jax.random.fold_in(jax.random.fold_in(own_key, 6), axis_at), (shards_of,), jnp.float32, low / len(cuts), largest / len(cuts))
        return jnp.repeat(jnp.exp(heights), extent[axis_at] // shards_of).reshape((-1,) + (1,) * (len(extent) - axis_at - 1))

    level = one(*cuts[0])
    for cut in cuts[1:]:
        level = level * one(*cut)
    return level


def assign_block(stream_key, own, number, rows, number_of, top, bound, skew):
    sequence = jax.random.permutation(stream_key, number_of)
    heavy_load, ordinary = load_shares(number_of, rows * top, bound, skew, True), load_shares(number_of, rows * top, bound, skew, False)
    places = jnp.arange(number_of)

    def named(tallies, turn):
        used = int((tallies > 0).sum())
        fixed = max(1, used // 4)
        moved = fixed + (places - fixed + turn * (used - fixed)) % max(1, number_of - fixed)
        return jnp.zeros((number_of,), jnp.int32).at[sequence[jnp.where(places < fixed, places, moved)]].set(jnp.asarray(tallies, jnp.int32))

    tallies = jnp.where(number % 4 == 0, named(heavy_load, number // 4), named(ordinary, number - number // 4 - 1))
    mixed = jax.random.permutation(jax.random.fold_in(own, 3), number_of)
    giver, receiver = mixed[0:number_of // 2 * 2:2], mixed[1:number_of // 2 * 2:2]
    slack = jnp.minimum(tallies[giver] - 1, bound - tallies[receiver]) // 2
    slack = jnp.where((giver == sequence[0]) | (receiver == sequence[0]) | (tallies[receiver] == 0), 0, jnp.maximum(slack, 0))
    moved = jax.random.randint(jax.random.fold_in(own, 4), (number_of // 2,), 0, 1 << 20) % (slack + 1)
    tallies = tallies.at[giver].add(-moved).at[receiver].add(moved)
    items = jnp.searchsorted(jnp.cumsum(tallies), jnp.arange(rows * top), side="right").astype(jnp.int32)
    table = items.reshape(top, rows).T
    table = table[jax.random.permutation(jax.random.fold_in(own, 1), rows)]
    turn = jax.random.randint(jax.random.fold_in(own, 2), (rows, 1), 0, top)
    return jnp.take_along_axis(table, (jnp.arange(top)[None, :] + turn) % top, axis=1)


def load_shares(number_of, total, limit, lean, full):
    weights = [(1 << 20) // math.isqrt(rank ** lean) + 1 for rank in range(1, number_of + 1)]
    largest = limit if full else min(limit, max(-(-total // number_of), total * weights[0] // sum(weights)))
    least = 1 if total - largest >= number_of - 1 else 0
    holding, rest = [largest] + [least] * (number_of - 1), total - largest - least * (number_of - 1)
    while rest > 0:
        candidates = [i for i in range(1, number_of) if holding[i] < largest] or [i for i in range(1, number_of) if holding[i] < limit]
        pool, remaining = sum([weights[i] for i in candidates]), rest
        for i in candidates:
            more = min(limit - holding[i], max(1, remaining * weights[i] // pool), rest)
            holding[i] = holding[i] + more
            rest = rest - more
    return np.array(holding)


def gaussian(own_key, extent, spread, most, cuts=(), kind=jnp.bfloat16):
    level = shard_levels(own_key, extent, cuts, -0.22, 0.18) if cuts else 1.0
    values = jax.random.normal(own_key, extent, jnp.float32) * spread * level
    return jnp.minimum(jnp.maximum(values, -most), most).astype(kind)


def setup_inputs(seed: int = 0) -> dict:
    splits = jax.random.split(jax.random.key(seed), 7)
    visibilities = gaussian(splits[0], (ROWS, 2 * CHAN), 1.0, 6.0, ((0, 128), (1, 2)))
    owner_tile_keys = jax.random.split(jax.random.fold_in(splits[1], 1), ROWS // ROWS_DEV)
    owner_tile_turns = jax.random.permutation(jax.random.fold_in(splits[1], 3), ROWS // ROWS_DEV)
    owner_tile = jax.vmap(lambda own, number: assign_block(jax.random.fold_in(splits[1], 2), own, number, ROWS_DEV, N_AU * N_VERT, 1, CAP, 2))(owner_tile_keys, owner_tile_turns).reshape((ROWS, 1))
    cell_row = with_ends(jax.random.randint(splits[2], (ROWS,), 0, TU), jax.random.fold_in(splits[2], 1), 0, TU - 1).astype(jnp.int32)
    cell_col = with_ends(jax.random.randint(splits[3], (ROWS,), 0, TV), jax.random.fold_in(splits[3], 1), 0, TV - 1).astype(jnp.int32)
    subcell = with_ends(jax.random.randint(splits[4], (2, ROWS), 0, OVS), jax.random.fold_in(splits[4], 1), 0, OVS - 1).astype(jnp.int32)
    channel_weight = jnp.clip(0.2 + 0.8 * jax.random.uniform(splits[5], (CHAN,), jnp.float32) ** shard_levels(splits[5], (CHAN,), ((0, 2),), -0.2, 0.2), 0.2, 1.0)
    return {"visibilities": visibilities, "owner_tile": owner_tile, "cell_row": cell_row, "cell_col": cell_col, "subcell": subcell, "channel_weight": channel_weight}


SIGMA = 1.5


def taper(distance):
    return jnp.exp(-distance * distance / (2.0 * SIGMA * SIGMA))


def reference(visibilities, owner_tile, cell_row, cell_col, subcell, channel_weight):
    row_count = visibilities.shape[0]
    column_count = visibilities.shape[1]
    margin = SUPPORT // 2 - 1
    tile_index = owner_tile[:, 0].astype(jnp.int32)
    base_row = ((tile_index // N_VERT) * TU + cell_row - margin).astype(jnp.int32)
    base_col = ((tile_index % N_VERT) * TV + cell_col - margin).astype(jnp.int32)
    tap_index = jnp.arange(SUPPORT, dtype=jnp.int32)
    tap_float = tap_index.astype(jnp.float32)
    taper_row = taper(tap_float[None, :] - float(margin) - subcell[0][:, None].astype(jnp.float32) / OVS)
    taper_col = taper(tap_float[None, :] - float(margin) - subcell[1][:, None].astype(jnp.float32) / OVS)
    block_rows = min(512, row_count)
    block_count = row_count // block_rows

    def split(array):
        return array.reshape((block_count, block_rows) + array.shape[1:])

    def accumulate(grid_flat, pieces):
        start_row, start_col, weight_row, weight_col, values = pieces
        product = (weight_row[:, :, None] * weight_col[:, None, :]).astype(jnp.bfloat16)
        product = lax.optimization_barrier(product).astype(jnp.float32)
        place_row = (start_row[:, None] + tap_index[None, :]) % NU
        place_col = (start_col[:, None] + tap_index[None, :]) % NV
        flat_index = (place_row[:, :, None] * NV + place_col[:, None, :]).reshape(-1).astype(jnp.int32)
        contrib = (product[:, :, :, None] * values.astype(jnp.float32)[:, None, None, :]).reshape(-1, column_count)
        return grid_flat.at[flat_index].add(contrib), None

    grid_flat = jnp.zeros((NU * NV, column_count), jnp.float32)
    grid_flat, ignored = lax.scan(accumulate, grid_flat, (split(base_row), split(base_col), split(taper_row), split(taper_col), split(visibilities)))
    grid = grid_flat.reshape(NU, NV, column_count)
    paired = grid.reshape(NU, NV, CHAN, 2)
    continuum = jnp.sum(paired * channel_weight[None, None, :, None], axis=2) / CHAN
    return grid, jnp.transpose(continuum, (2, 0, 1))
```

```python
import jax
import jax.numpy as jnp
from jax import lax
from jax.experimental import pallas as pl
from jax.experimental.pallas import tpu as pltpu
from jax.sharding import PartitionSpec as P

MESH = pl.DeviceIdType.MESH
F32 = jnp.float32
BF16 = jnp.bfloat16
I32 = jnp.int32

CHAN = 128
OVS = 8
SIGMA = 1.5
TU = 32
TV = 128
EU = TU + 8
EV = TV + 8
TILES = 128
CAP = 32
ROWS = 1024
COLS = 128
STEPS = 128
GROUP = 8
GROUPS = STEPS // GROUP
DEPTH = GROUP * CAP
UB = 4


def mod(value, by):
    return lax.rem(value + by, by)


def nt(lhs, rhs):
    return lax.dot_general(lhs, rhs, (((1,), (1,)), ((), ())), preferred_element_type=F32)


def nn(lhs, rhs):
    return jnp.dot(lhs, rhs, preferred_element_type=F32)


def flag(mask):
    return jnp.where(mask, 1.0, 0.0)


def kernel(
    vis_ref, tile_ref, pack_ref, weight_ref,
    grid_ref, cont_ref,
    acc, send_v, recv_v, send_m, recv_m, sid_ref, wr_ref, wc_ref,
    row_out, row_in, col_out, col_in, cor_out, cor_in, con_out, con_in,
    send_sem, recv_sem, msend_sem, mrecv_sem, hsend_sem, hrecv_sem, out_sem, line_sem,
):
    au, vert, ch = lax.axis_index("au"), lax.axis_index("vert"), lax.axis_index("ch")
    z, xl = lax.rem(vert, 8), vert // 8
    y, core = au // 2, lax.rem(au, 2)

    def target(group, dz):
        dc, dx, dy = lax.rem(group, 2), lax.rem(group // 2, 2), group // 4
        to_au = mod(y + dy, 4) * 2 + mod(core + dc, 2)
        to_vert = mod(xl + dx, 2) * 8 + mod(z + dz, 8)
        return to_au, to_vert

    barrier = pltpu.get_barrier_semaphore()

    def greet(to_au, to_vert, to_ch, sem):
        pl.semaphore_signal(sem, inc=1, device_id=(to_au, to_vert, to_ch), device_id_type=MESH)

    def greet_line(sem):
        def body(dz, carry):
            to_au, to_vert = target(0, dz)
            greet(to_au, to_vert, ch, sem)
            return carry
        lax.fori_loop(1, 8, body, 0)

    def greet_slab(group, carry):
        to_au, to_vert = target(group, 0)
        greet(to_au, to_vert, ch, barrier)
        return carry

    greet_line(barrier)
    lax.fori_loop(1, GROUPS, greet_slab, 0)
    greet(au, vert, 1 - ch, barrier)

    tile_row = tile_ref[...]
    packed_row = pack_ref[...]
    low = (packed_row & 63).astype(F32)
    middle = ((packed_row >> 6) & 127).astype(F32)
    high = (packed_row >> 13).astype(F32)
    strict = flag(
        lax.broadcasted_iota(I32, (128, 128), 0) < lax.broadcasted_iota(I32, (128, 128), 1)
    ).astype(BF16)
    sub_iota = lax.broadcasted_iota(I32, (128, 128), 0)
    lane_iota = lax.broadcasted_iota(I32, (128, 128), 1)
    ones = jnp.ones((128, 128), BF16)
    before = jnp.zeros((TILES, 128), F32)
    meta_low = jnp.zeros((TILES, 128), F32)
    meta_middle = jnp.zeros((TILES, 128), F32)
    meta_high = jnp.zeros((TILES, 128), F32)
    for part in range(ROWS // 128):
        cut = slice(part * 128, part * 128 + 128)
        hit = flag(sub_iota == tile_row[:, cut])
        hit_low = hit.astype(BF16)
        rank = nn(hit_low, strict) + before
        before = before + nn(hit_low, ones)
        place = jnp.sum(hit * rank, axis=0, keepdims=True).astype(I32)
        sid_ref[:, cut] = tile_row[:, cut] * CAP + place
        lane_hit = flag((sub_iota & (CAP - 1)) == place).astype(BF16)
        meta_low += nt((hit * low[:, cut]).astype(BF16), lane_hit)
        meta_middle += nt((hit * middle[:, cut]).astype(BF16), lane_hit)
        meta_high += nt((hit * high[:, cut]).astype(BF16), lane_hit)
    meta = meta_high * 8192.0 + meta_middle * 64.0 + meta_low
    quarter = lane_iota // CAP
    meta = jnp.where(quarter == lax.rem(sub_iota - z + 8, 4), meta, 0.0)
    send_m[...] = meta.reshape(TILES, 1, 128)
    acc[...] = jnp.zeros_like(acc)

    pl.semaphore_wait(barrier, 23)
    greet_line(line_sem)
    pl.semaphore_wait(line_sem, 7)

    def copies(group, dz):
        to_au, to_vert = target(group, dz)
        tile = to_au * 16 + to_vert
        step = group * GROUP + dz
        device = (to_au, to_vert, ch)
        return (
            pltpu.make_async_remote_copy(
                src_ref=send_v.at[tile], dst_ref=recv_v.at[step],
                send_sem=send_sem.at[step], recv_sem=recv_sem.at[step],
                device_id=device, device_id_type=MESH,
            ),
            pltpu.make_async_remote_copy(
                src_ref=send_m.at[tile], dst_ref=recv_m.at[step],
                send_sem=msend_sem.at[step], recv_sem=mrecv_sem.at[step],
                device_id=device, device_id_type=MESH,
            ),
        )

    def fill(group, first):
        to_au, to_vert = target(group, 0)
        base = to_au * 16 + (to_vert // 8) * 8
        slot = lax.broadcasted_iota(I32, (DEPTH, ROWS), 0) + base * CAP
        pick = flag(slot == sid_ref[...]).astype(BF16)
        send_v[pl.ds(base, GROUP)] = nn(pick, vis_ref[...]).astype(BF16).reshape(GROUP, CAP, COLS)

        def start(dz, carry):
            for copy in copies(group, dz):
                copy.start()
            return carry
        lax.fori_loop(first, GROUP, start, 0)

    fill(0, 1)
    mine = au * 16 + vert
    recv_v[0] = send_v[mine]
    recv_m[0] = send_m[mine]

    def fill_step(group, carry):
        fill(group, 0)
        return carry
    lax.fori_loop(1, GROUPS, fill_step, 0)

    def weights(meta_line):
        m = meta_line.astype(I32)
        a, b, o, p = m >> 13, (m >> 6) & 127, (m >> 3) & 7, m & 7

        def taper(index, extent, inner, cell, offset):
            cell_at = jnp.where(index < inner + 4, index, index - extent) - cell
            x = cell_at.astype(F32) - offset.astype(F32) / OVS
            tap = cell_at + 3
            return jnp.where((tap >= 0) & (tap < 8), jnp.exp(-x * x / (2.0 * SIGMA * SIGMA)), 0.0)

        wr_ref[...] = taper(lax.broadcasted_iota(I32, (EU, DEPTH), 0), EU, TU, a, o)
        wc_ref[...] = taper(lax.broadcasted_iota(I32, (EV, DEPTH), 0), EV, TV, b, p)

    def add_chunk(group):
        base = group * GROUP
        line = jnp.concatenate(
            [
                jnp.sum(recv_m[pl.ds(base, 4)].reshape(4, 128), axis=0, keepdims=True),
                jnp.sum(recv_m[pl.ds(base + 4, 4)].reshape(4, 128), axis=0, keepdims=True),
            ],
            axis=1,
        )
        weights(line)
        values = recv_v[pl.ds(base, GROUP)].reshape(DEPTH, COLS)

        def some(block, carry):
            u = block * UB
            col = wc_ref[...]
            taps = jnp.concatenate([col * wr_ref[pl.ds(u + i, 1), :] for i in range(UB)], axis=0)
            product = nn(taps.astype(BF16), values).reshape(UB, EV, COLS)
            acc[pl.ds(u, UB)] += product
            return carry
        lax.fori_loop(0, EU // UB, some, 0)

    def arrive(group, first):
        def body(dz, carry):
            for copy in copies(group, dz):
                copy.wait_recv()
            return carry
        lax.fori_loop(first, GROUP, body, 0)

    arrive(0, 1)
    add_chunk(0)

    def chunk_step(group, carry):
        arrive(group, 0)
        add_chunk(group)
        return carry
    lax.fori_loop(1, GROUPS, chunk_step, 0)

    row_out[...] = acc[TU:EU, 0:TV].reshape(2, 4 * TV, COLS).astype(BF16)
    col_out[...] = acc[0:TU, TV:EV].reshape(TU * 8, COLS).astype(BF16)
    cor_out[...] = acc[TU:EU, TV:EV].reshape(64, COLS).astype(BF16)
    down, up = mod(au + 1, 8), mod(au + 7, 8)
    right, left = mod(vert + 1, 16), mod(vert + 15, 16)

    def halo(src, dst, number, to_au, to_vert):
        return pltpu.make_async_remote_copy(
            src_ref=src, dst_ref=dst, send_sem=hsend_sem.at[number], recv_sem=hrecv_sem.at[number],
            device_id=(to_au, to_vert, ch), device_id_type=MESH,
        )

    halos = [
        halo(row_out.at[0], row_in.at[0], 0, down, vert),
        halo(row_out.at[1], row_in.at[1], 1, up, vert),
        halo(col_out, col_in.at[0], 2, au, right),
        halo(col_out, col_in.at[1], 3, au, left),
        halo(cor_out, cor_in.at[0], 4, down, right),
        halo(cor_out, cor_in.at[1], 5, down, left),
        halo(cor_out, cor_in.at[2], 6, up, right),
        halo(cor_out, cor_in.at[3], 7, up, left),
    ]
    for copy in halos:
        copy.start()

    def drain(group, first):
        def body(dz, carry):
            for copy in copies(group, dz):
                copy.wait_send()
            return carry
        lax.fori_loop(first, GROUP, body, 0)

    drain(0, 1)

    def drain_step(group, carry):
        drain(group, 0)
        return carry
    lax.fori_loop(1, GROUPS, drain_step, 0)

    for copy in halos:
        copy.wait()

    front = lax.broadcasted_iota(I32, (1, 8, COLS), 1) < 4
    acc[0:4, 0:TV] += row_in[0].astype(F32).reshape(4, TV, COLS)
    acc[TU - 4 : TU, 0:TV] += row_in[1].astype(F32).reshape(4, TV, COLS)
    from_left = col_in[0].astype(F32).reshape(TU, 8, COLS)
    from_right = col_in[1].astype(F32).reshape(TU, 8, COLS)
    acc[0:TU, 0:8] += jnp.where(front, from_left, 0.0)
    acc[0:TU, TV - 8 : TV] += jnp.where(front, 0.0, from_right)
    corners = [cor_in[i].astype(F32).reshape(8, 8, COLS) for i in range(4)]
    acc[0:4, 0:8] += jnp.where(front, corners[0][0:4], 0.0)
    acc[0:4, TV - 8 : TV] += jnp.where(front, 0.0, corners[1][0:4])
    acc[TU - 4 : TU, 0:8] += jnp.where(front, corners[2][4:8], 0.0)
    acc[TU - 4 : TU, TV - 8 : TV] += jnp.where(front, 0.0, corners[3][4:8])

    out = pltpu.make_async_copy(acc.at[pl.ds(0, TU), pl.ds(0, TV)], grid_ref, out_sem)
    out.start()

    weight = weight_ref[...]
    weight_high = weight.astype(BF16).astype(F32)
    weight_low = weight - weight_high
    kind = jnp.where(sub_iota < 64, weight_high, weight_low)
    result_at = (lane_iota & 1) * TU

    def channel_sum(u, total):
        cells = acc[pl.ds(u, 1), 0:TV].reshape(TV, COLS)
        cells_high = cells.astype(BF16)
        cells_low = (cells - cells_high.astype(F32)).astype(BF16)
        pick = jnp.where((sub_iota & 63) == result_at + u, kind, 0.0).astype(BF16)
        return total + nt(pick, cells_high) + nt(pick, cells_low)

    total = lax.fori_loop(0, TU, channel_sum, jnp.zeros((128, TV), F32))
    con_out[...] = total[0:64] + total[64:128]
    swap = pltpu.make_async_remote_copy(
        src_ref=con_out.at[pl.ds(pl.multiple_of((1 - ch) * TU, TU), TU)], dst_ref=con_in,
        send_sem=hsend_sem.at[8], recv_sem=hrecv_sem.at[8],
        device_id=(au, vert, 1 - ch), device_id_type=MESH,
    )
    swap.start()
    swap.wait()
    own = con_out[pl.ds(pl.multiple_of(ch * TU, TU), TU)]
    cont_ref[...] = (own + con_in[...]) * (1.0 / CHAN)
    out.wait()


def per_device(visibilities, owner_tile, cell_row, cell_col, subcell, channel_weight):
    tile = owner_tile.reshape(1, ROWS)
    packed = ((cell_row * TV + cell_col) * OVS + subcell[0]) * OVS + subcell[1]
    weight = jnp.repeat(channel_weight, 2).reshape(1, COLS)
    vmem = pl.BlockSpec(memory_space=pltpu.VMEM)
    grid, cont = pl.pallas_call(
        kernel,
        out_shape=(
            jax.ShapeDtypeStruct((TU, TV, COLS), F32),
            jax.ShapeDtypeStruct((TU, TV), F32),
        ),
        in_specs=[vmem] * 4,
        out_specs=(pl.BlockSpec(memory_space=pl.ANY), vmem),
        scratch_shapes=[
            pltpu.VMEM((EU, EV, COLS), F32),
            pltpu.VMEM((TILES, CAP, COLS), BF16),
            pltpu.VMEM((STEPS, CAP, COLS), BF16),
            pltpu.VMEM((TILES, 1, 128), F32),
            pltpu.VMEM((STEPS, 1, 128), F32),
            pltpu.VMEM((1, ROWS), I32),
            pltpu.VMEM((EU, DEPTH), F32),
            pltpu.VMEM((EV, DEPTH), F32),
            pltpu.VMEM((2, 4 * TV, COLS), BF16),
            pltpu.VMEM((2, 4 * TV, COLS), BF16),
            pltpu.VMEM((TU * 8, COLS), BF16),
            pltpu.VMEM((2, TU * 8, COLS), BF16),
            pltpu.VMEM((64, COLS), BF16),
            pltpu.VMEM((4, 64, COLS), BF16),
            pltpu.VMEM((2 * TU, TV), F32),
            pltpu.VMEM((TU, TV), F32),
            pltpu.SemaphoreType.DMA((STEPS,)),
            pltpu.SemaphoreType.DMA((STEPS,)),
            pltpu.SemaphoreType.DMA((STEPS,)),
            pltpu.SemaphoreType.DMA((STEPS,)),
            pltpu.SemaphoreType.DMA((9,)),
            pltpu.SemaphoreType.DMA((9,)),
            pltpu.SemaphoreType.DMA,
            pltpu.SemaphoreType.REGULAR,
        ],
        compiler_params=pltpu.CompilerParams(
            collective_id=0, has_side_effects=True, vmem_limit_bytes=40 * 2**20
        ),
        name="gridding",
    )(visibilities, tile, packed.reshape(1, ROWS), weight)
    return grid, cont.reshape(1, TU, TV)


def solution(mesh):
    in_specs = (
        P(("au", "vert"), "ch"),
        P(("au", "vert"), None),
        P(("au", "vert")),
        P(("au", "vert")),
        P(None, ("au", "vert")),
        P("ch"),
    )
    out_specs = (P("au", "vert", "ch"), P("ch", "au", "vert"))
    return jax.shard_map(
        per_device, mesh=mesh, in_specs=in_specs, out_specs=out_specs, check_vma=False
    )
```

```python
import jax
import jax.numpy as jnp
from jax import lax
from jax.experimental import pallas as pl
from jax.experimental.pallas import tpu as pltpu
from jax.sharding import PartitionSpec as P

MESH = pl.DeviceIdType.MESH
F32 = jnp.float32
BF16 = jnp.bfloat16
I32 = jnp.int32

CHAN = 128
OVS = 8
SIGMA = 1.5
TU = 32
TV = 128
EU = TU + 8
EV = TV + 8
TILES = 128
CAP = 32
ROWS = 1024
COLS = 128
STEPS = 128
GROUP = 8
GROUPS = STEPS // GROUP
DEPTH = GROUP * CAP
UB = 4
EARLY = 4


def mod(value, by):
    return lax.rem(value + by, by)


def nt(lhs, rhs):
    return lax.dot_general(lhs, rhs, (((1,), (1,)), ((), ())), preferred_element_type=F32)


def nn(lhs, rhs):
    return jnp.dot(lhs, rhs, preferred_element_type=F32)


def flag(mask):
    return jnp.where(mask, 1.0, 0.0)


def kernel(
    vis_hbm, tile_hbm, row_hbm, col_hbm, sub_hbm, weight_hbm,
    grid_hbm, cont_hbm,
    vis_ref, tile_ref, cell_row_ref, cell_col_ref, sub_ref, weight_ref, grid_ref, cont_ref,
    col_acc, row_acc, send_v, recv_v, send_m, recv_m, sid_ref, wr_ref, wc_ref,
    row_out, row_in, col_out, col_in, cor_out, cor_in,
    sum_main, sum_edge, sum_mid_in, sum_row_in, sum_col_in, sum_cor_in,
    load_sem, store_sem, send_sem, recv_sem, hsend_sem, hrecv_sem, ssend_sem, srecv_sem, line_sem, twin_sem,
):
    au, vert, ch = lax.axis_index("au"), lax.axis_index("vert"), lax.axis_index("ch")
    z, xl = lax.rem(vert, 8), vert // 8
    y, core = au // 2, lax.rem(au, 2)

    def target(group, dz):
        dc, dx, dy = lax.rem(group, 2), lax.rem(group // 2, 2), group // 4
        to_au = mod(y + dy, 4) * 2 + mod(core + dc, 2)
        to_vert = mod(xl + dx, 2) * 8 + mod(z + dz, 8)
        return to_au, to_vert

    loads = [
        pltpu.make_async_copy(src, dst, load_sem.at[i])
        for i, (src, dst) in enumerate([
            (tile_hbm, tile_ref), (row_hbm, cell_row_ref), (col_hbm, cell_col_ref),
            (sub_hbm, sub_ref), (weight_hbm, weight_ref), (vis_hbm, vis_ref),
        ])
    ]
    for load in loads:
        load.start()
    barrier = pltpu.get_barrier_semaphore()

    def greet(to_au, to_vert, to_ch, sem):
        pl.semaphore_signal(sem, inc=1, device_id=(to_au, to_vert, to_ch), device_id_type=MESH)

    def greet_line(sem):
        for dz in range(1, 8):
            greet(*target(0, dz), ch, sem)

    greet_line(barrier)
    for group in range(1, GROUPS):
        greet(*target(group, 0), ch, barrier)
    greet(au, vert, 1 - ch, barrier)
    grid_ref[...] = jnp.zeros_like(grid_ref)
    col_acc[...] = jnp.zeros_like(col_acc)
    row_acc[...] = jnp.zeros_like(row_acc)
    sum_edge[...] = jnp.zeros_like(sum_edge)
    for load in loads:
        load.wait()

    tile_row = tile_ref[...]
    low = (sub_ref[0:1, :] * OVS + sub_ref[1:2, :]).astype(F32)
    middle = cell_col_ref[...].astype(F32)
    high = cell_row_ref[...].astype(F32)
    strict = flag(
        lax.broadcasted_iota(I32, (128, 128), 0) < lax.broadcasted_iota(I32, (128, 128), 1)
    ).astype(BF16)
    sub_iota = lax.broadcasted_iota(I32, (128, 128), 0)
    lane_iota = lax.broadcasted_iota(I32, (128, 128), 1)
    ones = jnp.ones((128, 128), BF16)
    before = jnp.zeros((TILES, 128), F32)
    meta_low = jnp.zeros((TILES, 128), F32)
    meta_middle = jnp.zeros((TILES, 128), F32)
    meta_high = jnp.zeros((TILES, 128), F32)
    for part in range(ROWS // 128):
        cut = slice(part * 128, part * 128 + 128)
        hit = flag(sub_iota == tile_row[:, cut])
        hit_low = hit.astype(BF16)
        rank = nn(hit_low, strict) + before
        before = before + nn(hit_low, ones)
        place = jnp.sum(hit * rank, axis=0, keepdims=True).astype(I32)
        sid_ref[:, cut] = tile_row[:, cut] * CAP + place
        lane_hit = flag((sub_iota & (CAP - 1)) == place).astype(BF16)
        meta_low += nt((hit * low[:, cut]).astype(BF16), lane_hit)
        meta_middle += nt((hit * middle[:, cut]).astype(BF16), lane_hit)
        meta_high += nt((hit * high[:, cut]).astype(BF16), lane_hit)
    meta = meta_high * 8192.0 + meta_middle * 64.0 + meta_low
    quarter = lane_iota // CAP
    meta = jnp.where(quarter == lax.rem(sub_iota - z + 8, 4), meta, 0.0)
    send_m[...] = meta.reshape(TILES, 1, 128)

    def copies(group, dz):
        to_au, to_vert = target(group, dz)
        tile = to_au * 16 + to_vert
        step = group * GROUP + dz
        device = (to_au, to_vert, ch)
        return [
            pltpu.make_async_remote_copy(
                src_ref=src.at[tile], dst_ref=dst.at[step],
                send_sem=send_sem.at[kind], recv_sem=recv_sem.at[kind, group],
                device_id=device, device_id_type=MESH,
            )
            for kind, (src, dst) in enumerate([(send_v, recv_v), (send_m, recv_m)])
        ]

    def fill(group):
        to_au, to_vert = target(group, 0)
        base = to_au * 16 + (to_vert // 8) * 8
        slot = lax.broadcasted_iota(I32, (DEPTH, ROWS), 0) + base * CAP
        pick = flag(slot == sid_ref[...]).astype(BF16)
        send_v[pl.ds(base, GROUP)] = nn(pick, vis_ref[...]).astype(BF16).reshape(GROUP, CAP, COLS)

    def start(group, first):
        for dz in range(first, GROUP):
            for copy in copies(group, dz):
                copy.start()

    pl.semaphore_wait(barrier, 23)
    greet_line(line_sem)
    fill(0)
    start(0, 1)
    mine = au * 16 + vert
    recv_v[0] = send_v[mine]
    recv_m[0] = send_m[mine]
    for group in range(1, EARLY):
        fill(group)
    pl.semaphore_wait(line_sem, 7)
    greet(au, vert, 1 - ch, twin_sem)
    for group in range(1, EARLY):
        start(group, 0)

    def fill_step(group, carry):
        fill(group)
        start(group, 0)
        return carry
    lax.fori_loop(EARLY, GROUPS, fill_step, 0)

    def weights(meta_line):
        m = meta_line.astype(I32)
        a, b, o, p = m >> 13, (m >> 6) & 127, (m >> 3) & 7, m & 7

        def taper(index, extent, inner, cell, offset):
            cell_at = jnp.where(index < inner + 4, index, index - extent) - cell
            x = cell_at.astype(F32) - offset.astype(F32) / OVS
            tap = cell_at + 3
            return jnp.where((tap >= 0) & (tap < 8), jnp.exp(-x * x / (2.0 * SIGMA * SIGMA)), 0.0)

        depth = m.shape[1]
        wr_ref[:, 0:depth] = taper(lax.broadcasted_iota(I32, (EU, depth), 0), EU, TU, a, o)
        wc_ref[:, 0:depth] = taper(lax.broadcasted_iota(I32, (EV, depth), 0), EV, TV, b, p)

    def arrived(group, first, count):
        span = pl.ds(group * GROUP + first, count)
        for kind, ref in enumerate([recv_v, recv_m]):
            pltpu.make_async_copy(ref.at[span], ref.at[span], recv_sem.at[kind, group]).wait()

    def add_chunk(group, groups, after_rows):
        base = group * GROUP
        depth = groups * DEPTH
        line = jnp.concatenate(
            [
                jnp.sum(recv_m[pl.ds(base + 4 * i, 4)].reshape(4, 128), axis=0, keepdims=True)
                for i in range(2 * groups)
            ],
            axis=1,
        )
        weights(line)
        values = recv_v[pl.ds(base, groups * GROUP)].reshape(depth, COLS)
        for u in [*range(TU, EU, UB), *range(0, TU, UB)]:
            if u == 0:
                after_rows()
            col = wc_ref[:, 0:depth]
            taps = jnp.concatenate([col * wr_ref[u + i : u + i + 1, 0:depth] for i in range(UB)], axis=0)
            product = nn(taps.astype(BF16), values).reshape(UB, EV, COLS)
            if u < TU:
                grid_ref[u : u + UB] += product[:, 0:TV]
                col_acc[u : u + UB] += product[:, TV:EV]
            else:
                row_acc[u - TU : u - TU + UB] += product

    arrived(0, 1, GROUP - 1)
    add_chunk(0, 1, lambda: None)

    def chunk_step(pair, carry):
        group = 2 * pair + 1
        arrived(group, 0, GROUP)
        arrived(group + 1, 0, GROUP)
        add_chunk(group, 2, lambda: None)
        return carry
    lax.fori_loop(0, GROUPS // 2 - 1, chunk_step, 0)
    down, up = mod(au + 1, 8), mod(au + 7, 8)
    right, left = mod(vert + 1, 16), mod(vert + 15, 16)

    def halo(src, dst, number, to_au, to_vert):
        return pltpu.make_async_remote_copy(
            src_ref=src, dst_ref=dst, send_sem=hsend_sem.at[number], recv_sem=hrecv_sem.at[number],
            device_id=(to_au, to_vert, ch), device_id_type=MESH,
        )

    row_halos = [
        halo(row_out.at[0], row_in.at[0], 0, down, vert),
        halo(row_out.at[1], row_in.at[1], 1, up, vert),
        halo(cor_out, cor_in.at[0], 2, down, right),
        halo(cor_out, cor_in.at[1], 3, down, left),
        halo(cor_out, cor_in.at[2], 4, up, right),
        halo(cor_out, cor_in.at[3], 5, up, left),
    ]
    col_halos = [
        halo(col_out, col_in.at[0], 6, au, right),
        halo(col_out, col_in.at[1], 7, au, left),
    ]

    def send_rows():
        row_out[...] = row_acc[:, 0:TV].reshape(2, 4 * TV, COLS).astype(BF16)
        cor_out[...] = row_acc[:, TV:EV].reshape(64, COLS).astype(BF16)
        for copy in row_halos:
            copy.start()

    arrived(GROUPS - 1, 0, GROUP)
    add_chunk(GROUPS - 1, 1, send_rows)
    col_out[...] = col_acc[...].reshape(TU * 8, COLS).astype(BF16)
    for copy in col_halos:
        copy.start()

    spread = flag(
        lax.broadcasted_iota(I32, (COLS // 2, COLS), 0) == lax.broadcasted_iota(I32, (COLS // 2, COLS), 1) // 2
    ).astype(BF16)
    weight = jnp.zeros((1, COLS), F32)
    rest = weight_ref[...]
    for part in range(3):
        piece = rest.astype(BF16)
        rest = rest - piece.astype(F32)
        weight += nn(piece, spread)
    weight_high = weight.astype(BF16).astype(F32)
    line = lax.broadcasted_iota(I32, (16, COLS), 0)
    mine_only = (line & 1) == (lax.broadcasted_iota(I32, (16, COLS), 1) & 1)
    pick = jnp.where(line < 2, weight_high, jnp.where(line < 4, weight - weight_high, 0.0))
    pick = jnp.where(mine_only, pick, 0.0).astype(BF16)
    pick = jnp.concatenate([pick, pick], axis=1)

    def channel_sum(u):
        if u < TU:
            cells = jnp.concatenate([grid_ref[u], col_acc[u]], axis=0)
        else:
            cells = row_acc[u - TU]
        cells_high = cells.astype(BF16)
        cells_low = (cells - cells_high.astype(F32)).astype(BF16)
        result = nt(pick, jnp.concatenate([cells_high, cells_low], axis=1))
        return result[0:2] + result[2:4]

    for u in range(0, EU, 8):
        sums = [channel_sum(u + i) for i in range(8)]
        for q in range(2):
            whole = jnp.concatenate([one[q : q + 1] for one in sums], axis=0)
            sum_main[q, u : u + 8, :] = whole[:, 0:TV]
            sum_edge[q, u : u + 8, 0:8] = whole[:, TV:EV]

    def part(src, dst, number, to_au, to_vert, to_ch):
        return pltpu.make_async_remote_copy(
            src_ref=src, dst_ref=dst, send_sem=ssend_sem.at[number], recv_sem=srecv_sem.at[number],
            device_id=(to_au, to_vert, to_ch), device_id_type=MESH,
        )

    parts = [part(sum_main.at[1 - ch, pl.ds(0, TU)], sum_mid_in, 0, au, vert, 1 - ch)]
    for other in range(2):
        q = 1 - ch if other else ch
        rows, cols, edge = pl.ds(TU, 8), pl.ds(0, TU), 1 + 8 * other
        parts += [
            part(sum_main.at[q, rows], sum_row_in.at[other, 0], edge, down, vert, q),
            part(sum_main.at[q, rows], sum_row_in.at[other, 1], edge + 1, up, vert, q),
            part(sum_edge.at[q, cols], sum_col_in.at[other, 0], edge + 2, au, right, q),
            part(sum_edge.at[q, cols], sum_col_in.at[other, 1], edge + 3, au, left, q),
            part(sum_edge.at[q, rows], sum_cor_in.at[other, 0], edge + 4, down, right, q),
            part(sum_edge.at[q, rows], sum_cor_in.at[other, 1], edge + 5, down, left, q),
            part(sum_edge.at[q, rows], sum_cor_in.at[other, 2], edge + 6, up, right, q),
            part(sum_edge.at[q, rows], sum_cor_in.at[other, 3], edge + 7, up, left, q),
        ]
    pl.semaphore_wait(twin_sem, 1)
    for copy in parts:
        copy.start()

    for kind, ref in enumerate([recv_v, recv_m]):
        span = pl.ds(1, STEPS - 1)
        pltpu.make_async_copy(ref.at[span], ref.at[span], send_sem.at[kind]).wait()
    for copy in row_halos + col_halos:
        copy.wait()

    front = lax.broadcasted_iota(I32, (1, 8, COLS), 1) < 4
    grid_ref[0:4, 0:TV] += row_in[0].astype(F32).reshape(4, TV, COLS)
    grid_ref[TU - 4 : TU, 0:TV] += row_in[1].astype(F32).reshape(4, TV, COLS)
    from_left = col_in[0].astype(F32).reshape(TU, 8, COLS)
    from_right = col_in[1].astype(F32).reshape(TU, 8, COLS)
    grid_ref[0:TU, 0:8] += jnp.where(front, from_left, 0.0)
    grid_ref[0:TU, TV - 8 : TV] += jnp.where(front, 0.0, from_right)
    corners = [cor_in[i].astype(F32).reshape(8, 8, COLS) for i in range(4)]
    grid_ref[0:4, 0:8] += jnp.where(front, corners[0][0:4], 0.0)
    grid_ref[0:4, TV - 8 : TV] += jnp.where(front, 0.0, corners[1][0:4])
    grid_ref[TU - 4 : TU, 0:8] += jnp.where(front, corners[2][4:8], 0.0)
    grid_ref[TU - 4 : TU, TV - 8 : TV] += jnp.where(front, 0.0, corners[3][4:8])

    stores = [
        pltpu.make_async_copy(grid_ref.at[pl.ds(u, 8)], grid_hbm.at[pl.ds(u, 8)], store_sem.at[u // 8])
        for u in range(0, TU, 8)
    ]
    for store in stores:
        store.start()
    for copy in parts:
        copy.wait()
    top = lax.broadcasted_iota(I32, (8, TV), 0) < 4
    lane = lax.broadcasted_iota(I32, (TU, TV), 1)

    def sides(from_left, from_right, rows):
        at = lane[0:rows]
        return jnp.where(at < 4, from_left, 0.0) + jnp.where(at >= TV - 4, pltpu.roll(from_right, TV - 8, 1), 0.0)

    total = sum_main[ch, 0:TU] + sum_mid_in[...]
    first = jnp.zeros((8, TV), F32)
    last = jnp.zeros((8, TV), F32)
    for other in range(2):
        total += sides(sum_col_in[other, 0], sum_col_in[other, 1], TU)
        first += sum_row_in[other, 0] + sides(sum_cor_in[other, 0], sum_cor_in[other, 1], 8)
        last += sum_row_in[other, 1] + sides(sum_cor_in[other, 2], sum_cor_in[other, 3], 8)
    cont_ref[...] = total * (1.0 / CHAN)
    cont_ref[0:8] += jnp.where(top, first, 0.0) * (1.0 / CHAN)
    cont_ref[TU - 8 : TU] += jnp.where(top, 0.0, last) * (1.0 / CHAN)
    store = pltpu.make_async_copy(cont_ref, cont_hbm, store_sem.at[4])
    store.start()
    for store in [*stores, store]:
        store.wait()


def handover(grid_in, cont_in, grid_out, cont_out, grid_ref, cont_ref, in_sem, out_sem):
    cuts = [pl.ds(u, 4) for u in range(0, TU, 4)]
    spots = [(grid_in.at[cut], grid_ref.at[cut], grid_out.at[cut]) for cut in cuts]
    spots.append((cont_in, cont_ref, cont_out))
    takes = [pltpu.make_async_copy(src, via, in_sem.at[i]) for i, (src, via, dst) in enumerate(spots)]
    gives = [pltpu.make_async_copy(via, dst, out_sem.at[i]) for i, (src, via, dst) in enumerate(spots)]
    for take in takes:
        take.start()
    for take, give in zip(takes, gives):
        take.wait()
        give.start()
    for give in gives:
        give.wait()


def per_device(visibilities, owner_tile, cell_row, cell_col, subcell, channel_weight):
    anywhere = pl.BlockSpec(memory_space=pl.ANY)
    shapes = (jax.ShapeDtypeStruct((TU, TV, COLS), F32), jax.ShapeDtypeStruct((TU, TV), F32))
    grid, cont = pl.pallas_call(
        kernel,
        out_shape=shapes,
        in_specs=[anywhere] * 6,
        out_specs=(anywhere, anywhere),
        scratch_shapes=[
            pltpu.VMEM((ROWS, COLS), BF16),
            pltpu.VMEM((1, ROWS), I32),
            pltpu.VMEM((1, ROWS), I32),
            pltpu.VMEM((1, ROWS), I32),
            pltpu.VMEM((2, ROWS), I32),
            pltpu.VMEM((1, COLS // 2), F32),
            pltpu.VMEM((TU, TV, COLS), F32),
            pltpu.VMEM((TU, TV), F32),
            pltpu.VMEM((TU, 8, COLS), F32),
            pltpu.VMEM((8, EV, COLS), F32),
            pltpu.VMEM((TILES, CAP, COLS), BF16),
            pltpu.VMEM((STEPS, CAP, COLS), BF16),
            pltpu.VMEM((TILES, 1, 128), F32),
            pltpu.VMEM((STEPS, 1, 128), F32),
            pltpu.VMEM((1, ROWS), I32),
            pltpu.VMEM((EU, 2 * DEPTH), F32),
            pltpu.VMEM((EV, 2 * DEPTH), F32),
            pltpu.VMEM((2, 4 * TV, COLS), BF16),
            pltpu.VMEM((2, 4 * TV, COLS), BF16),
            pltpu.VMEM((TU * 8, COLS), BF16),
            pltpu.VMEM((2, TU * 8, COLS), BF16),
            pltpu.VMEM((64, COLS), BF16),
            pltpu.VMEM((4, 64, COLS), BF16),
            pltpu.VMEM((2, EU, TV), F32),
            pltpu.VMEM((2, EU, TV), F32),
            pltpu.VMEM((TU, TV), F32),
            pltpu.VMEM((2, 2, 8, TV), F32),
            pltpu.VMEM((2, 2, TU, TV), F32),
            pltpu.VMEM((2, 4, 8, TV), F32),
            pltpu.SemaphoreType.DMA((6,)),
            pltpu.SemaphoreType.DMA((5,)),
            pltpu.SemaphoreType.DMA((2,)),
            pltpu.SemaphoreType.DMA((2, GROUPS)),
            pltpu.SemaphoreType.DMA((8,)),
            pltpu.SemaphoreType.DMA((8,)),
            pltpu.SemaphoreType.DMA((17,)),
            pltpu.SemaphoreType.DMA((17,)),
            pltpu.SemaphoreType.REGULAR,
            pltpu.SemaphoreType.REGULAR,
        ],
        compiler_params=pltpu.CompilerParams(
            collective_id=0, has_side_effects=True, vmem_limit_bytes=62 * 2**20
        ),
        name="gridding",
    )(
        visibilities, owner_tile.reshape(1, ROWS), cell_row.reshape(1, ROWS),
        cell_col.reshape(1, ROWS), subcell, channel_weight.reshape(1, COLS // 2),
    )
    grid, cont = pl.pallas_call(
        handover,
        out_shape=shapes,
        in_specs=[anywhere] * 2,
        out_specs=(anywhere, anywhere),
        scratch_shapes=[
            pltpu.VMEM((TU, TV, COLS), F32),
            pltpu.VMEM((TU, TV), F32),
            pltpu.SemaphoreType.DMA((9,)),
            pltpu.SemaphoreType.DMA((9,)),
        ],
        compiler_params=pltpu.CompilerParams(vmem_limit_bytes=62 * 2**20),
        name="handover",
    )(grid, cont)
    return grid, cont.reshape(1, TU, TV)


def solution(mesh):
    in_specs = (
        P(("au", "vert"), "ch"),
        P(("au", "vert"), None),
        P(("au", "vert")),
        P(("au", "vert")),
        P(None, ("au", "vert")),
        P("ch"),
    )
    out_specs = (P("au", "vert", "ch"), P("ch", "au", "vert"))
    return jax.shard_map(
        per_device, mesh=mesh, in_specs=in_specs, out_specs=out_specs, check_vma=False
    )
```

```python
import jax
import jax.numpy as jnp
from jax import lax
from jax.experimental import pallas as pl
from jax.experimental.pallas import tpu as pltpu
from jax.sharding import PartitionSpec as P

MESH = pl.DeviceIdType.MESH
F32 = jnp.float32
BF16 = jnp.bfloat16
I32 = jnp.int32

CHAN = 128
OVS = 8
SIGMA = 1.5
TU = 32
TV = 128
EU = TU + 8
EV = TV + 8
TILES = 128
CAP = 32
ROWS = 1024
COLS = 128
STEPS = 128
GROUP = 8
GROUPS = STEPS // GROUP
DEPTH = GROUP * CAP
UB = 4


def mod(value, by):
    return lax.rem(value + by, by)


def nt(lhs, rhs):
    return lax.dot_general(lhs, rhs, (((1,), (1,)), ((), ())), preferred_element_type=F32)


def nn(lhs, rhs):
    return jnp.dot(lhs, rhs, preferred_element_type=F32)


def flag(mask):
    return jnp.where(mask, 1.0, 0.0)


def kernel(
    vis_hbm, tile_hbm, row_hbm, col_hbm, sub_hbm, weight_hbm,
    grid_hbm, cont_hbm,
    vis_ref, tile_ref, cell_row_ref, cell_col_ref, sub_ref, weight_ref, grid_ref, cont_ref,
    col_acc, row_acc, send_v, recv_v, send_m, recv_m, sid_ref, wr_ref, wc_ref,
    row_out, row_in, col_out, col_in, cor_out, cor_in,
    sums, sum_row_in, sum_col_in, sum_cor_in, twin_out, twin_in,
    load_sem, store_sem, send_sem, recv_sem, hsend_sem, hrecv_sem, ssend_sem, srecv_sem, twin_sem, stack_sem,
):
    au, vert, ch = lax.axis_index("au"), lax.axis_index("vert"), lax.axis_index("ch")
    z, xl = lax.rem(vert, 8), vert // 8
    y, core = au // 2, lax.rem(au, 2)

    def target(group, dz):
        dx, dc, dy = lax.rem(group, 2), lax.rem(group // 2, 2), group // 4
        to_au = mod(y + dy, 4) * 2 + mod(core + dc, 2)
        to_vert = mod(xl + dx, 2) * 8 + mod(z + dz, 8)
        return to_au, to_vert

    loads = [
        pltpu.make_async_copy(src, dst, load_sem.at[i])
        for i, (src, dst) in enumerate([
            (tile_hbm, tile_ref), (row_hbm, cell_row_ref), (col_hbm, cell_col_ref),
            (sub_hbm, sub_ref), (weight_hbm, weight_ref), (vis_hbm, vis_ref),
        ])
    ]
    for load in loads:
        load.start()
    barrier = pltpu.get_barrier_semaphore()

    def greet(to_au, to_vert, to_ch, sem):
        pl.semaphore_signal(sem, inc=1, device_id=(to_au, to_vert, to_ch), device_id_type=MESH)

    def greet_stack(sem):
        for group in range(2, GROUPS, 2):
            greet(*target(group, 0), ch, sem)

    for step in range(1, 2 * GROUP):
        greet(*target(step // GROUP, step % GROUP), ch, barrier)
    greet_stack(barrier)
    greet(au, vert, 1 - ch, barrier)
    for load in loads:
        load.wait()

    tile_row = tile_ref[...]
    strict = flag(
        lax.broadcasted_iota(I32, (128, 128), 0) < lax.broadcasted_iota(I32, (128, 128), 1)
    ).astype(BF16)
    sub_iota = lax.broadcasted_iota(I32, (128, 128), 0)
    lane_iota = lax.broadcasted_iota(I32, (128, 128), 1)
    ones = jnp.ones((128, 128), BF16)
    before = jnp.zeros((TILES, 128), F32)
    for part in range(ROWS // 128):
        cut = slice(part * 128, part * 128 + 128)
        hit = flag(sub_iota == tile_row[:, cut])
        hit_low = hit.astype(BF16)
        rank = nn(hit_low, strict) + before
        before = before + nn(hit_low, ones)
        place = jnp.sum(hit * rank, axis=0, keepdims=True).astype(I32)
        sid_ref[:, cut] = tile_row[:, cut] * CAP + place

    spread = flag(
        lax.broadcasted_iota(I32, (COLS // 2, COLS), 0) == lax.broadcasted_iota(I32, (COLS // 2, COLS), 1) // 2
    ).astype(BF16)

    def thirds(values):
        pieces = []
        for _ in range(3):
            pieces.append(values.astype(BF16))
            values = values - pieces[-1].astype(F32)
        return pieces

    weight = sum(nn(piece, spread) for piece in thirds(weight_ref[...]))
    line = lax.broadcasted_iota(I32, (16, COLS), 0)
    mine_only = (line & 1) == (lax.broadcasted_iota(I32, (16, COLS), 1) & 1)
    pick = jnp.zeros((16, COLS), F32)
    for i, piece in enumerate(thirds(weight)):
        pick = jnp.where(mine_only & (line // 2 == i), piece.astype(F32), pick)
    both = nt(pick.astype(BF16), vis_ref[...])
    twin_out[...] = (both[0:2] + both[2:4] + both[4:6]).reshape(2, 1, ROWS)
    swap = pltpu.make_async_remote_copy(
        src_ref=twin_out.at[1 - ch], dst_ref=twin_in, send_sem=twin_sem.at[0], recv_sem=twin_sem.at[1],
        device_id=(au, vert, 1 - ch), device_id_type=MESH,
    )

    def copy_of(kind, group, dz):
        to_au, to_vert = target(group, dz)
        tile = to_au * 16 + to_vert
        step = group * GROUP + dz
        device = (to_au, to_vert, ch)
        src, dst = [(send_v, recv_v), (send_m, recv_m)][kind]
        return pltpu.make_async_remote_copy(
            src_ref=src.at[tile], dst_ref=dst.at[step],
            send_sem=send_sem.at[kind], recv_sem=recv_sem.at[kind, group],
            device_id=device, device_id_type=MESH,
        )

    def fill(group):
        to_au, to_vert = target(group, 0)
        base = to_au * 16 + (to_vert // 8) * 8
        slot = lax.broadcasted_iota(I32, (DEPTH, ROWS), 0) + base * CAP
        pick = flag(slot == sid_ref[...]).astype(BF16)
        send_v[pl.ds(base, GROUP)] = nn(pick, vis_ref[...]).astype(BF16).reshape(GROUP, CAP, COLS)

    def start(kind, group, first):
        for dz in range(first, GROUP):
            copy_of(kind, group, dz).start()

    fill(0)
    pl.semaphore_wait(barrier, 23)
    greet_stack(stack_sem)
    start(0, 0, 1)
    swap.start()
    fill(1)
    start(0, 1, 0)
    mine = au * 16 + vert
    recv_v[0] = send_v[mine]
    fill(2)
    fill(3)
    pl.semaphore_wait(stack_sem, 7)
    start(0, 2, 0)
    start(0, 3, 0)

    low = (sub_ref[0:1, :] * OVS + sub_ref[1:2, :]).astype(F32)
    middle = cell_col_ref[...].astype(F32)
    high = cell_row_ref[...].astype(F32)
    swap.wait()
    fields = [high, middle, low]
    fields += [piece.astype(F32) for piece in thirds(twin_out[ch] + twin_in[...])]
    slots = jnp.zeros((len(fields) * TILES, 128), F32)
    for part in range(ROWS // 128):
        cut = slice(part * 128, part * 128 + 128)
        hit = flag(sub_iota == tile_row[:, cut])
        lane_hit = flag((sub_iota & (CAP - 1)) == (sid_ref[:, cut] & (CAP - 1))).astype(BF16)
        slots += nt(jnp.concatenate([hit * field[:, cut] for field in fields], axis=0).astype(BF16), lane_hit)
    slots = [slots[i * TILES : i * TILES + TILES] for i in range(len(fields))]
    meta = slots[0] * 8192.0 + slots[1] * 64.0 + slots[2]
    quarter = lane_iota // CAP
    turn = lax.rem(sub_iota - z + 8, 4)
    meta = jnp.where(quarter == turn, meta, 0.0)
    meta = jnp.where(quarter == ((turn + 1) & 3), slots[3] + slots[4] + slots[5], meta)
    send_m[...] = meta.reshape(TILES, 1, 128)
    recv_m[0] = send_m[mine]
    for group in range(4):
        start(1, group, 1 if group == 0 else 0)
    grid_ref[...] = jnp.zeros_like(grid_ref)
    col_acc[...] = jnp.zeros_like(col_acc)
    row_acc[...] = jnp.zeros_like(row_acc)
    sums[...] = jnp.zeros_like(sums)

    def fill_step(group, carry):
        fill(group)
        start(0, group, 0)
        start(1, group, 0)
        return carry
    lax.fori_loop(4, GROUPS, fill_step, 0)

    def weights(meta_line):
        m = meta_line.astype(I32)
        a, b, o, p = m >> 13, (m >> 6) & 127, (m >> 3) & 7, m & 7

        def taper(index, extent, inner, cell, offset):
            cell_at = jnp.where(index < inner + 4, index, index - extent) - cell
            x = cell_at.astype(F32) - offset.astype(F32) / OVS
            tap = cell_at + 3
            return jnp.where((tap >= 0) & (tap < 8), jnp.exp(-x * x / (2.0 * SIGMA * SIGMA)), 0.0)

        depth = m.shape[1]
        wr_ref[:, 0:depth] = taper(lax.broadcasted_iota(I32, (EU, depth), 0), EU, TU, a, o)
        wc_ref[:, 0:depth] = taper(lax.broadcasted_iota(I32, (EV, depth), 0), EV, TV, b, p)

    def arrived(group, first, count):
        span = pl.ds(group * GROUP + first, count)
        for kind, ref in enumerate([recv_v, recv_m]):
            pltpu.make_async_copy(ref.at[span], ref.at[span], recv_sem.at[kind, group]).wait()

    def add_chunk(group, groups, before_rows, after_rows):
        base = group * GROUP
        depth = groups * DEPTH
        quarter = lax.broadcasted_iota(I32, (4, 128), 1) // CAP == lax.broadcasted_iota(I32, (4, 128), 0)
        metas, totals = [], []
        for i in range(2 * groups):
            lines = recv_m[pl.ds(base + 4 * i, 4)].reshape(4, 128)
            metas.append(jnp.sum(jnp.where(quarter, lines, 0.0), axis=0, keepdims=True))
            lines = pltpu.roll(lines, 128 - CAP, 1)
            totals.append(jnp.sum(jnp.where(quarter, lines, 0.0), axis=0, keepdims=True))
        weights(jnp.concatenate(metas, axis=1))
        left_high, left_low, _ = thirds(wr_ref[:, 0:depth] * jnp.concatenate(totals, axis=1))
        right_high, right_low, _ = thirds(wc_ref[:, 0:depth])
        sums[:, 0:EV] += nt(left_high, right_high) + nt(left_low, right_high) + nt(left_high, right_low)
        before_rows()
        values = recv_v[pl.ds(base, groups * GROUP)].reshape(depth, COLS)
        for u in [*range(TU, EU, UB), *range(0, TU, UB)]:
            if u == 0:
                after_rows()
            col = wc_ref[:, 0:depth]
            taps = jnp.concatenate([col * wr_ref[u + i : u + i + 1, 0:depth] for i in range(UB)], axis=0)
            product = nn(taps.astype(BF16), values).reshape(UB, EV, COLS)
            if u < TU:
                grid_ref[u : u + UB] += product[:, 0:TV]
                col_acc[u : u + UB] += product[:, TV:EV]
            else:
                row_acc[u - TU : u - TU + UB] += product

    arrived(0, 1, GROUP - 1)
    add_chunk(0, 1, lambda: None, lambda: None)

    def chunk_step(pair, carry):
        group = 2 * pair + 1
        arrived(group, 0, GROUP)
        arrived(group + 1, 0, GROUP)
        add_chunk(group, 2, lambda: None, lambda: None)
        return carry
    lax.fori_loop(0, GROUPS // 2 - 1, chunk_step, 0)
    down, up = mod(au + 1, 8), mod(au + 7, 8)
    right, left = mod(vert + 1, 16), mod(vert + 15, 16)

    def halo(src, dst, number, to_au, to_vert):
        return pltpu.make_async_remote_copy(
            src_ref=src, dst_ref=dst, send_sem=hsend_sem.at[number], recv_sem=hrecv_sem.at[number],
            device_id=(to_au, to_vert, ch), device_id_type=MESH,
        )

    row_halos = [
        halo(row_out.at[0], row_in.at[0], 0, down, vert),
        halo(row_out.at[1], row_in.at[1], 1, up, vert),
        halo(cor_out, cor_in.at[0], 2, down, right),
        halo(cor_out, cor_in.at[1], 3, down, left),
        halo(cor_out, cor_in.at[2], 4, up, right),
        halo(cor_out, cor_in.at[3], 5, up, left),
    ]
    col_halos = [
        halo(col_out, col_in.at[0], 6, au, right),
        halo(col_out, col_in.at[1], 7, au, left),
    ]

    def send_rows():
        row_out[...] = row_acc[:, 0:TV].reshape(2, 4 * TV, COLS).astype(BF16)
        cor_out[...] = row_acc[:, TV:EV].reshape(64, COLS).astype(BF16)
        for copy in row_halos:
            copy.start()

    def part(src, dst, number, to_au, to_vert):
        return pltpu.make_async_remote_copy(
            src_ref=src, dst_ref=dst, send_sem=ssend_sem.at[number], recv_sem=srecv_sem.at[number],
            device_id=(to_au, to_vert, ch), device_id_type=MESH,
        )

    row_sums = sums.at[pl.ds(TU, 8), pl.ds(0, TV)]
    col_sums = sums.at[pl.ds(0, TU), pl.ds(TV, TV)]
    cor_sums = sums.at[pl.ds(TU, 8), pl.ds(TV, TV)]
    parts = [
        part(row_sums, sum_row_in.at[0], 0, down, vert),
        part(row_sums, sum_row_in.at[1], 1, up, vert),
        part(col_sums, sum_col_in.at[0], 2, au, right),
        part(col_sums, sum_col_in.at[1], 3, au, left),
        part(cor_sums, sum_cor_in.at[0], 4, down, right),
        part(cor_sums, sum_cor_in.at[1], 5, down, left),
        part(cor_sums, sum_cor_in.at[2], 6, up, right),
        part(cor_sums, sum_cor_in.at[3], 7, up, left),
    ]

    def send_sums():
        for copy in parts:
            copy.start()

    arrived(GROUPS - 1, 0, GROUP)
    add_chunk(GROUPS - 1, 1, send_sums, send_rows)
    col_out[...] = col_acc[...].reshape(TU * 8, COLS).astype(BF16)
    for copy in col_halos:
        copy.start()

    for kind, ref in enumerate([recv_v, recv_m]):
        span = pl.ds(1, STEPS - 1)
        pltpu.make_async_copy(ref.at[span], ref.at[span], send_sem.at[kind]).wait()
    for copy in row_halos + col_halos:
        copy.wait()

    front = lax.broadcasted_iota(I32, (1, 8, COLS), 1) < 4
    grid_ref[0:4, 0:TV] += row_in[0].astype(F32).reshape(4, TV, COLS)
    grid_ref[TU - 4 : TU, 0:TV] += row_in[1].astype(F32).reshape(4, TV, COLS)
    from_left = col_in[0].astype(F32).reshape(TU, 8, COLS)
    from_right = col_in[1].astype(F32).reshape(TU, 8, COLS)
    grid_ref[0:TU, 0:8] += jnp.where(front, from_left, 0.0)
    grid_ref[0:TU, TV - 8 : TV] += jnp.where(front, 0.0, from_right)
    corners = [cor_in[i].astype(F32).reshape(8, 8, COLS) for i in range(4)]
    grid_ref[0:4, 0:8] += jnp.where(front, corners[0][0:4], 0.0)
    grid_ref[0:4, TV - 8 : TV] += jnp.where(front, 0.0, corners[1][0:4])
    grid_ref[TU - 4 : TU, 0:8] += jnp.where(front, corners[2][4:8], 0.0)
    grid_ref[TU - 4 : TU, TV - 8 : TV] += jnp.where(front, 0.0, corners[3][4:8])

    stores = [
        pltpu.make_async_copy(grid_ref.at[pl.ds(u, 8)], grid_hbm.at[pl.ds(u, 8)], store_sem.at[u // 8])
        for u in range(0, TU, 8)
    ]
    for store in stores:
        store.start()
    for copy in parts:
        copy.wait()
    top = lax.broadcasted_iota(I32, (8, TV), 0) < 4
    lane = lax.broadcasted_iota(I32, (TU, TV), 1)

    def sides(from_left, from_right, rows):
        at = lane[0:rows]
        return jnp.where(at < 4, from_left, 0.0) + jnp.where(at >= TV - 4, pltpu.roll(from_right, TV - 8, 1), 0.0)

    total = sums[0:TU, 0:TV] + sides(sum_col_in[0], sum_col_in[1], TU)
    first = sum_row_in[0] + sides(sum_cor_in[0], sum_cor_in[1], 8)
    last = sum_row_in[1] + sides(sum_cor_in[2], sum_cor_in[3], 8)
    cont_ref[...] = total * (1.0 / CHAN)
    cont_ref[0:8] += jnp.where(top, first, 0.0) * (1.0 / CHAN)
    cont_ref[TU - 8 : TU] += jnp.where(top, 0.0, last) * (1.0 / CHAN)
    store = pltpu.make_async_copy(cont_ref, cont_hbm, store_sem.at[4])
    store.start()
    for store in [*stores, store]:
        store.wait()


def handover(grid_in, cont_in, grid_out, cont_out, grid_ref, cont_ref, in_sem, out_sem):
    cuts = [pl.ds(u, 4) for u in range(0, TU, 4)]
    spots = [(grid_in.at[cut], grid_ref.at[cut], grid_out.at[cut]) for cut in cuts]
    spots.append((cont_in, cont_ref, cont_out))
    takes = [pltpu.make_async_copy(src, via, in_sem.at[i]) for i, (src, via, dst) in enumerate(spots)]
    gives = [pltpu.make_async_copy(via, dst, out_sem.at[i]) for i, (src, via, dst) in enumerate(spots)]
    for take in takes:
        take.start()
    for take, give in zip(takes, gives):
        take.wait()
        give.start()
    for give in gives:
        give.wait()


def per_device(visibilities, owner_tile, cell_row, cell_col, subcell, channel_weight):
    anywhere = pl.BlockSpec(memory_space=pl.ANY)
    shapes = (jax.ShapeDtypeStruct((TU, TV, COLS), F32), jax.ShapeDtypeStruct((TU, TV), F32))
    grid, cont = pl.pallas_call(
        kernel,
        out_shape=shapes,
        in_specs=[anywhere] * 6,
        out_specs=(anywhere, anywhere),
        scratch_shapes=[
            pltpu.VMEM((ROWS, COLS), BF16),
            pltpu.VMEM((1, ROWS), I32),
            pltpu.VMEM((1, ROWS), I32),
            pltpu.VMEM((1, ROWS), I32),
            pltpu.VMEM((2, ROWS), I32),
            pltpu.VMEM((1, COLS // 2), F32),
            pltpu.VMEM((TU, TV, COLS), F32),
            pltpu.VMEM((TU, TV), F32),
            pltpu.VMEM((TU, 8, COLS), F32),
            pltpu.VMEM((8, EV, COLS), F32),
            pltpu.VMEM((TILES, CAP, COLS), BF16),
            pltpu.VMEM((STEPS, CAP, COLS), BF16),
            pltpu.VMEM((TILES, 1, 128), F32),
            pltpu.VMEM((STEPS, 1, 128), F32),
            pltpu.VMEM((1, ROWS), I32),
            pltpu.VMEM((EU, 2 * DEPTH), F32),
            pltpu.VMEM((EV, 2 * DEPTH), F32),
            pltpu.VMEM((2, 4 * TV, COLS), BF16),
            pltpu.VMEM((2, 4 * TV, COLS), BF16),
            pltpu.VMEM((TU * 8, COLS), BF16),
            pltpu.VMEM((2, TU * 8, COLS), BF16),
            pltpu.VMEM((64, COLS), BF16),
            pltpu.VMEM((4, 64, COLS), BF16),
            pltpu.VMEM((EU, 2 * TV), F32),
            pltpu.VMEM((2, 8, TV), F32),
            pltpu.VMEM((2, TU, TV), F32),
            pltpu.VMEM((4, 8, TV), F32),
            pltpu.VMEM((2, 1, ROWS), F32),
            pltpu.VMEM((1, ROWS), F32),
            pltpu.SemaphoreType.DMA((6,)),
            pltpu.SemaphoreType.DMA((5,)),
            pltpu.SemaphoreType.DMA((2,)),
            pltpu.SemaphoreType.DMA((2, GROUPS)),
            pltpu.SemaphoreType.DMA((8,)),
            pltpu.SemaphoreType.DMA((8,)),
            pltpu.SemaphoreType.DMA((8,)),
            pltpu.SemaphoreType.DMA((8,)),
            pltpu.SemaphoreType.DMA((2,)),
            pltpu.SemaphoreType.REGULAR,
        ],
        compiler_params=pltpu.CompilerParams(
            collective_id=0, has_side_effects=True, vmem_limit_bytes=62 * 2**20
        ),
        name="gridding",
    )(
        visibilities, owner_tile.reshape(1, ROWS), cell_row.reshape(1, ROWS),
        cell_col.reshape(1, ROWS), subcell, channel_weight.reshape(1, COLS // 2),
    )
    grid, cont = pl.pallas_call(
        handover,
        out_shape=shapes,
        in_specs=[anywhere] * 2,
        out_specs=(anywhere, anywhere),
        scratch_shapes=[
            pltpu.VMEM((TU, TV, COLS), F32),
            pltpu.VMEM((TU, TV), F32),
            pltpu.SemaphoreType.DMA((9,)),
            pltpu.SemaphoreType.DMA((9,)),
        ],
        compiler_params=pltpu.CompilerParams(vmem_limit_bytes=62 * 2**20),
        name="handover",
    )(grid, cont)
    return grid, cont.reshape(1, TU, TV)


def solution(mesh):
    in_specs = (
        P(("au", "vert"), "ch"),
        P(("au", "vert"), None),
        P(("au", "vert")),
        P(("au", "vert")),
        P(None, ("au", "vert")),
        P("ch"),
    )
    out_specs = (P("au", "vert", "ch"), P("ch", "au", "vert"))
    return jax.shard_map(
        per_device, mesh=mesh, in_specs=in_specs, out_specs=out_specs, check_vma=False
    )
```

```python
import jax
import jax.numpy as jnp
from jax import lax
from jax.experimental import pallas as pl
from jax.experimental.pallas import tpu as pltpu
from jax.sharding import PartitionSpec as P

MESH = pl.DeviceIdType.MESH
F32 = jnp.float32
BF16 = jnp.bfloat16
I32 = jnp.int32

CHAN = 128
OVS = 8
SIGMA = 1.5
TU = 32
TV = 128
EU = TU + 8
EV = TV + 8
TILES = 128
CAP = 32
ROWS = 1024
COLS = 128
STEPS = 128
GROUP = 8
GROUPS = STEPS // GROUP
DEPTH = GROUP * CAP
UB = 4


def mod(value, by):
    return lax.rem(value + by, by)


def nt(lhs, rhs):
    return lax.dot_general(lhs, rhs, (((1,), (1,)), ((), ())), preferred_element_type=F32)


def nn(lhs, rhs):
    return jnp.dot(lhs, rhs, preferred_element_type=F32)


def flag(mask):
    return jnp.where(mask, 1.0, 0.0)


def kernel(
    vis_hbm, tile_hbm, row_hbm, col_hbm, sub_hbm, weight_hbm,
    grid_hbm, cont_hbm,
    vis_ref, tile_ref, cell_row_ref, cell_col_ref, sub_ref, weight_ref, grid_ref, cont_ref,
    col_acc, row_acc, send_v, recv_v, send_m, recv_m, sid_ref, wr_ref, wc_ref,
    row_out, row_in, col_out, col_in, cor_out, cor_in,
    sums, sum_row_in, sum_col_in, sum_cor_in, twin_out, twin_in,
    load_sem, store_sem, send_sem, recv_sem, hsend_sem, hrecv_sem, ssend_sem, srecv_sem, twin_sem, stack_sem,
):
    au, vert, ch = lax.axis_index("au"), lax.axis_index("vert"), lax.axis_index("ch")
    z, xl = lax.rem(vert, 8), vert // 8
    y, core = au // 2, lax.rem(au, 2)

    def target(group, dz):
        dx, dc, dy = lax.rem(group, 2), lax.rem(group // 2, 2), group // 4
        to_au = mod(y + dy, 4) * 2 + mod(core + dc, 2)
        to_vert = mod(xl + dx, 2) * 8 + mod(z + dz, 8)
        return to_au, to_vert

    loads = [
        pltpu.make_async_copy(src, dst, load_sem.at[i])
        for i, (src, dst) in enumerate([
            (tile_hbm, tile_ref), (row_hbm, cell_row_ref), (col_hbm, cell_col_ref),
            (sub_hbm, sub_ref), (weight_hbm, weight_ref), (vis_hbm, vis_ref),
        ])
    ]
    for load in loads:
        load.start()
    barrier = pltpu.get_barrier_semaphore()

    def greet(to_au, to_vert, to_ch, sem):
        pl.semaphore_signal(sem, inc=1, device_id=(to_au, to_vert, to_ch), device_id_type=MESH)

    def greet_stack(sem):
        for group in range(2, GROUPS, 2):
            greet(*target(group, 0), ch, sem)

    for step in range(1, 2 * GROUP):
        greet(*target(step // GROUP, step % GROUP), ch, barrier)
    greet_stack(barrier)
    greet(au, vert, 1 - ch, barrier)
    for load in loads:
        load.wait()

    tile_row = tile_ref[...]
    strict = flag(
        lax.broadcasted_iota(I32, (128, 128), 0) < lax.broadcasted_iota(I32, (128, 128), 1)
    ).astype(BF16)
    sub_iota = lax.broadcasted_iota(I32, (128, 128), 0)
    lane_iota = lax.broadcasted_iota(I32, (128, 128), 1)
    ones = jnp.ones((128, 128), BF16)
    before = jnp.zeros((TILES, 128), F32)
    for part in range(ROWS // 128):
        cut = slice(part * 128, part * 128 + 128)
        hit = flag(sub_iota == tile_row[:, cut])
        hit_low = hit.astype(BF16)
        rank = nn(hit_low, strict) + before
        before = before + nn(hit_low, ones)
        place = jnp.sum(hit * rank, axis=0, keepdims=True).astype(I32)
        sid_ref[:, cut] = tile_row[:, cut] * CAP + place

    spread = flag(
        lax.broadcasted_iota(I32, (COLS // 2, COLS), 0) == lax.broadcasted_iota(I32, (COLS // 2, COLS), 1) // 2
    ).astype(BF16)

    def thirds(values):
        pieces = []
        for _ in range(3):
            pieces.append(values.astype(BF16))
            values = values - pieces[-1].astype(F32)
        return pieces

    weight = sum(nn(piece, spread) for piece in thirds(weight_ref[...]))
    line = lax.broadcasted_iota(I32, (16, COLS), 0)
    mine_only = (line & 1) == (lax.broadcasted_iota(I32, (16, COLS), 1) & 1)
    pick = jnp.zeros((16, COLS), F32)
    for i, piece in enumerate(thirds(weight)):
        pick = jnp.where(mine_only & (line // 2 == i), piece.astype(F32), pick)
    both = nt(pick.astype(BF16), vis_ref[...])
    twin_out[...] = (both[0:2] + both[2:4] + both[4:6]).reshape(2, 1, ROWS)
    swap = pltpu.make_async_remote_copy(
        src_ref=twin_out.at[1 - ch], dst_ref=twin_in, send_sem=twin_sem.at[0], recv_sem=twin_sem.at[1],
        device_id=(au, vert, 1 - ch), device_id_type=MESH,
    )

    def copy_of(kind, group, dz):
        to_au, to_vert = target(group, dz)
        tile = to_au * 16 + to_vert
        step = group * GROUP + dz
        device = (to_au, to_vert, ch)
        src, dst = [(send_v, recv_v), (send_m, recv_m)][kind]
        return pltpu.make_async_remote_copy(
            src_ref=src.at[tile], dst_ref=dst.at[step],
            send_sem=send_sem.at[kind], recv_sem=recv_sem.at[kind, group],
            device_id=device, device_id_type=MESH,
        )

    def fill(group):
        to_au, to_vert = target(group, 0)
        base = to_au * 16 + (to_vert // 8) * 8
        slot = lax.broadcasted_iota(I32, (DEPTH, ROWS), 0) + base * CAP
        pick = flag(slot == sid_ref[...]).astype(BF16)
        send_v[pl.ds(base, GROUP)] = nn(pick, vis_ref[...]).astype(BF16).reshape(GROUP, CAP, COLS)

    def start(kind, group, first):
        for dz in range(first, GROUP):
            copy_of(kind, group, dz).start()

    fill(0)
    pl.semaphore_wait(barrier, 23)
    greet_stack(stack_sem)
    start(0, 0, 1)
    swap.start()
    fill(1)
    start(0, 1, 0)
    mine = au * 16 + vert
    recv_v[0] = send_v[mine]
    fill(2)
    fill(3)
    pl.semaphore_wait(stack_sem, 7)
    start(0, 2, 0)
    start(0, 3, 0)

    low = (sub_ref[0:1, :] * OVS + sub_ref[1:2, :]).astype(F32)
    middle = cell_col_ref[...].astype(F32)
    high = cell_row_ref[...].astype(F32)
    swap.wait()
    fields = [high, middle, low]
    fields += [piece.astype(F32) for piece in thirds(twin_out[ch] + twin_in[...])]
    slots = jnp.zeros((len(fields) * TILES, 128), F32)
    for part in range(ROWS // 128):
        cut = slice(part * 128, part * 128 + 128)
        hit = flag(sub_iota == tile_row[:, cut])
        lane_hit = flag((sub_iota & (CAP - 1)) == (sid_ref[:, cut] & (CAP - 1))).astype(BF16)
        slots += nt(jnp.concatenate([hit * field[:, cut] for field in fields], axis=0).astype(BF16), lane_hit)
    slots = [slots[i * TILES : i * TILES + TILES] for i in range(len(fields))]
    meta = slots[0] * 8192.0 + slots[1] * 64.0 + slots[2]
    quarter = lane_iota // CAP
    turn = lax.rem(sub_iota - z + 8, 4)
    meta = jnp.where(quarter == turn, meta, 0.0)
    meta = jnp.where(quarter == ((turn + 1) & 3), slots[3] + slots[4] + slots[5], meta)
    send_m[...] = meta.reshape(TILES, 1, 128)
    recv_m[0] = send_m[mine]
    for group in range(4):
        start(1, group, 1 if group == 0 else 0)
    grid_ref[...] = jnp.zeros_like(grid_ref)
    col_acc[...] = jnp.zeros_like(col_acc)
    row_acc[...] = jnp.zeros_like(row_acc)
    sums[...] = jnp.zeros_like(sums)

    def fill_step(group, carry):
        fill(group)
        start(0, group, 0)
        start(1, group, 0)
        return carry
    lax.fori_loop(4, GROUPS, fill_step, 0)

    def weights(meta_line):
        m = meta_line.astype(I32)
        a, b, o, p = m >> 13, (m >> 6) & 127, (m >> 3) & 7, m & 7

        def taper(index, extent, inner, cell, offset):
            cell_at = jnp.where(index < inner + 4, index, index - extent) - cell
            x = cell_at.astype(F32) - offset.astype(F32) / OVS
            tap = cell_at + 3
            return jnp.where((tap >= 0) & (tap < 8), jnp.exp(-x * x / (2.0 * SIGMA * SIGMA)), 0.0)

        depth = m.shape[1]
        wr_ref[:, 0:depth] = taper(lax.broadcasted_iota(I32, (EU, depth), 0), EU, TU, a, o)
        wc_ref[:, 0:depth] = taper(lax.broadcasted_iota(I32, (EV, depth), 0), EV, TV, b, p)

    def arrived(group, first, count):
        span = pl.ds(group * GROUP + first, count)
        for kind, ref in enumerate([recv_v, recv_m]):
            pltpu.make_async_copy(ref.at[span], ref.at[span], recv_sem.at[kind, group]).wait()

    def add_chunk(group, groups, before_rows, after_rows):
        base = group * GROUP
        depth = groups * DEPTH
        quarter = lax.broadcasted_iota(I32, (4, 128), 1) // CAP == lax.broadcasted_iota(I32, (4, 128), 0)
        metas, totals = [], []
        for i in range(2 * groups):
            lines = recv_m[pl.ds(base + 4 * i, 4)].reshape(4, 128)
            metas.append(jnp.sum(jnp.where(quarter, lines, 0.0), axis=0, keepdims=True))
            lines = pltpu.roll(lines, 128 - CAP, 1)
            totals.append(jnp.sum(jnp.where(quarter, lines, 0.0), axis=0, keepdims=True))
        weights(jnp.concatenate(metas, axis=1))
        left_high, left_low, _ = thirds(wr_ref[:, 0:depth] * jnp.concatenate(totals, axis=1))
        right_high, right_low, _ = thirds(wc_ref[:, 0:depth])
        sums[:, 0:EV] += nt(left_high, right_high) + nt(left_low, right_high) + nt(left_high, right_low)
        before_rows()
        values = recv_v[pl.ds(base, groups * GROUP)].reshape(depth, COLS)
        for u in [*range(TU, EU, UB), *range(0, TU, UB)]:
            if u == 0:
                after_rows()
            col = wc_ref[:, 0:depth]
            taps = jnp.concatenate([col * wr_ref[u + i : u + i + 1, 0:depth] for i in range(UB)], axis=0)
            product = nn(taps.astype(BF16), values).reshape(UB, EV, COLS)
            if u < TU:
                grid_ref[u : u + UB] += product[:, 0:TV]
                col_acc[u : u + UB] += product[:, TV:EV]
            else:
                row_acc[u - TU : u - TU + UB] += product

    arrived(0, 1, GROUP - 1)
    add_chunk(0, 1, lambda: None, lambda: None)

    def chunk_step(pair, carry):
        group = 2 * pair + 1
        arrived(group, 0, GROUP)
        arrived(group + 1, 0, GROUP)
        add_chunk(group, 2, lambda: None, lambda: None)
        return carry
    lax.fori_loop(0, GROUPS // 2 - 1, chunk_step, 0)
    down, up = mod(au + 1, 8), mod(au + 7, 8)
    right, left = mod(vert + 1, 16), mod(vert + 15, 16)

    def halo(src, dst, number, to_au, to_vert):
        return pltpu.make_async_remote_copy(
            src_ref=src, dst_ref=dst, send_sem=hsend_sem.at[number], recv_sem=hrecv_sem.at[number],
            device_id=(to_au, to_vert, ch), device_id_type=MESH,
        )

    row_halos = [
        halo(row_out.at[0], row_in.at[0], 0, down, vert),
        halo(row_out.at[1], row_in.at[1], 1, up, vert),
        halo(cor_out, cor_in.at[0], 2, down, right),
        halo(cor_out, cor_in.at[1], 3, down, left),
        halo(cor_out, cor_in.at[2], 4, up, right),
        halo(cor_out, cor_in.at[3], 5, up, left),
    ]
    col_halos = [
        halo(col_out, col_in.at[0], 6, au, right),
        halo(col_out, col_in.at[1], 7, au, left),
    ]

    def send_rows():
        row_out[...] = row_acc[:, 0:TV].reshape(2, 4 * TV, COLS).astype(BF16)
        cor_out[...] = row_acc[:, TV:EV].reshape(64, COLS).astype(BF16)
        for copy in row_halos:
            copy.start()

    def part(src, dst, number, to_au, to_vert):
        return pltpu.make_async_remote_copy(
            src_ref=src, dst_ref=dst, send_sem=ssend_sem.at[number], recv_sem=srecv_sem.at[number],
            device_id=(to_au, to_vert, ch), device_id_type=MESH,
        )

    row_sums = sums.at[pl.ds(TU, 8), pl.ds(0, TV)]
    col_sums = sums.at[pl.ds(0, TU), pl.ds(TV, TV)]
    cor_sums = sums.at[pl.ds(TU, 8), pl.ds(TV, TV)]
    parts = [
        part(row_sums, sum_row_in.at[0], 0, down, vert),
        part(row_sums, sum_row_in.at[1], 1, up, vert),
        part(col_sums, sum_col_in.at[0], 2, au, right),
        part(col_sums, sum_col_in.at[1], 3, au, left),
        part(cor_sums, sum_cor_in.at[0], 4, down, right),
        part(cor_sums, sum_cor_in.at[1], 5, down, left),
        part(cor_sums, sum_cor_in.at[2], 6, up, right),
        part(cor_sums, sum_cor_in.at[3], 7, up, left),
    ]

    def send_sums():
        for copy in parts:
            copy.start()

    arrived(GROUPS - 1, 0, GROUP)
    add_chunk(GROUPS - 1, 1, send_sums, send_rows)
    col_out[...] = col_acc[...].reshape(TU * 8, COLS).astype(BF16)
    for copy in col_halos:
        copy.start()

    inner_rows = pl.ds(4, TU - 8)
    blocks = [
        (inner_rows, pl.ds(8, TV - 16)),
        (pl.ds(0, 4), pl.ds(0, TV)),
        (pl.ds(TU - 4, 4), pl.ds(0, TV)),
        (inner_rows, pl.ds(0, 8)),
        (inner_rows, pl.ds(TV - 8, 8)),
    ]
    stores = [
        pltpu.make_async_copy(grid_ref.at[block], grid_hbm.at[block], store_sem.at[i])
        for i, block in enumerate(blocks)
    ]
    stores[0].start()

    for kind, ref in enumerate([recv_v, recv_m]):
        span = pl.ds(1, STEPS - 1)
        pltpu.make_async_copy(ref.at[span], ref.at[span], send_sem.at[kind]).wait()
    for copy in row_halos + col_halos:
        copy.wait()

    front = lax.broadcasted_iota(I32, (1, 8, COLS), 1) < 4
    grid_ref[0:4, 0:TV] += row_in[0].astype(F32).reshape(4, TV, COLS)
    grid_ref[TU - 4 : TU, 0:TV] += row_in[1].astype(F32).reshape(4, TV, COLS)
    from_left = col_in[0].astype(F32).reshape(TU, 8, COLS)
    from_right = col_in[1].astype(F32).reshape(TU, 8, COLS)
    grid_ref[0:TU, 0:8] += jnp.where(front, from_left, 0.0)
    grid_ref[0:TU, TV - 8 : TV] += jnp.where(front, 0.0, from_right)
    corners = [cor_in[i].astype(F32).reshape(8, 8, COLS) for i in range(4)]
    grid_ref[0:4, 0:8] += jnp.where(front, corners[0][0:4], 0.0)
    grid_ref[0:4, TV - 8 : TV] += jnp.where(front, 0.0, corners[1][0:4])
    grid_ref[TU - 4 : TU, 0:8] += jnp.where(front, corners[2][4:8], 0.0)
    grid_ref[TU - 4 : TU, TV - 8 : TV] += jnp.where(front, 0.0, corners[3][4:8])

    for store in stores[1:]:
        store.start()
    for copy in parts:
        copy.wait()
    top = lax.broadcasted_iota(I32, (8, TV), 0) < 4
    lane = lax.broadcasted_iota(I32, (TU, TV), 1)

    def sides(from_left, from_right, rows):
        at = lane[0:rows]
        return jnp.where(at < 4, from_left, 0.0) + jnp.where(at >= TV - 4, pltpu.roll(from_right, TV - 8, 1), 0.0)

    total = sums[0:TU, 0:TV] + sides(sum_col_in[0], sum_col_in[1], TU)
    first = sum_row_in[0] + sides(sum_cor_in[0], sum_cor_in[1], 8)
    last = sum_row_in[1] + sides(sum_cor_in[2], sum_cor_in[3], 8)
    cont_ref[...] = total * (1.0 / CHAN)
    cont_ref[0:8] += jnp.where(top, first, 0.0) * (1.0 / CHAN)
    cont_ref[TU - 8 : TU] += jnp.where(top, 0.0, last) * (1.0 / CHAN)
    store = pltpu.make_async_copy(cont_ref, cont_hbm, store_sem.at[5])
    store.start()
    for store in [*stores, store]:
        store.wait()


def handover(grid_in, cont_in, grid_out, cont_out, grid_ref, cont_ref, in_sem, out_sem):
    cuts = [pl.ds(u, 4) for u in range(0, TU, 4)]
    spots = [(grid_in.at[cut], grid_ref.at[cut], grid_out.at[cut]) for cut in cuts]
    spots.append((cont_in, cont_ref, cont_out))
    takes = [pltpu.make_async_copy(src, via, in_sem.at[i]) for i, (src, via, dst) in enumerate(spots)]
    gives = [pltpu.make_async_copy(via, dst, out_sem.at[i]) for i, (src, via, dst) in enumerate(spots)]
    for take in takes:
        take.start()
    for take, give in zip(takes, gives):
        take.wait()
        give.start()
    for give in gives:
        give.wait()


def per_device(visibilities, owner_tile, cell_row, cell_col, subcell, channel_weight):
    anywhere = pl.BlockSpec(memory_space=pl.ANY)
    shapes = (jax.ShapeDtypeStruct((TU, TV, COLS), F32), jax.ShapeDtypeStruct((TU, TV), F32))
    grid, cont = pl.pallas_call(
        kernel,
        out_shape=shapes,
        in_specs=[anywhere] * 6,
        out_specs=(anywhere, anywhere),
        scratch_shapes=[
            pltpu.VMEM((ROWS, COLS), BF16),
            pltpu.VMEM((1, ROWS), I32),
            pltpu.VMEM((1, ROWS), I32),
            pltpu.VMEM((1, ROWS), I32),
            pltpu.VMEM((2, ROWS), I32),
            pltpu.VMEM((1, COLS // 2), F32),
            pltpu.VMEM((TU, TV, COLS), F32),
            pltpu.VMEM((TU, TV), F32),
            pltpu.VMEM((TU, 8, COLS), F32),
            pltpu.VMEM((8, EV, COLS), F32),
            pltpu.VMEM((TILES, CAP, COLS), BF16),
            pltpu.VMEM((STEPS, CAP, COLS), BF16),
            pltpu.VMEM((TILES, 1, 128), F32),
            pltpu.VMEM((STEPS, 1, 128), F32),
            pltpu.VMEM((1, ROWS), I32),
            pltpu.VMEM((EU, 2 * DEPTH), F32),
            pltpu.VMEM((EV, 2 * DEPTH), F32),
            pltpu.VMEM((2, 4 * TV, COLS), BF16),
            pltpu.VMEM((2, 4 * TV, COLS), BF16),
            pltpu.VMEM((TU * 8, COLS), BF16),
            pltpu.VMEM((2, TU * 8, COLS), BF16),
            pltpu.VMEM((64, COLS), BF16),
            pltpu.VMEM((4, 64, COLS), BF16),
            pltpu.VMEM((EU, 2 * TV), F32),
            pltpu.VMEM((2, 8, TV), F32),
            pltpu.VMEM((2, TU, TV), F32),
            pltpu.VMEM((4, 8, TV), F32),
            pltpu.VMEM((2, 1, ROWS), F32),
            pltpu.VMEM((1, ROWS), F32),
            pltpu.SemaphoreType.DMA((6,)),
            pltpu.SemaphoreType.DMA((6,)),
            pltpu.SemaphoreType.DMA((2,)),
            pltpu.SemaphoreType.DMA((2, GROUPS)),
            pltpu.SemaphoreType.DMA((8,)),
            pltpu.SemaphoreType.DMA((8,)),
            pltpu.SemaphoreType.DMA((8,)),
            pltpu.SemaphoreType.DMA((8,)),
            pltpu.SemaphoreType.DMA((2,)),
            pltpu.SemaphoreType.REGULAR,
        ],
        compiler_params=pltpu.CompilerParams(
            collective_id=0, has_side_effects=True, vmem_limit_bytes=62 * 2**20
        ),
        name="gridding",
    )(
        visibilities, owner_tile.reshape(1, ROWS), cell_row.reshape(1, ROWS),
        cell_col.reshape(1, ROWS), subcell, channel_weight.reshape(1, COLS // 2),
    )
    grid, cont = pl.pallas_call(
        handover,
        out_shape=shapes,
        in_specs=[anywhere] * 2,
        out_specs=(anywhere, anywhere),
        scratch_shapes=[
            pltpu.VMEM((TU, TV, COLS), F32),
            pltpu.VMEM((TU, TV), F32),
            pltpu.SemaphoreType.DMA((9,)),
            pltpu.SemaphoreType.DMA((9,)),
        ],
        compiler_params=pltpu.CompilerParams(vmem_limit_bytes=62 * 2**20),
        name="handover",
    )(grid, cont)
    return grid, cont.reshape(1, TU, TV)


def solution(mesh):
    in_specs = (
        P(("au", "vert"), "ch"),
        P(("au", "vert"), None),
        P(("au", "vert")),
        P(("au", "vert")),
        P(None, ("au", "vert")),
        P("ch"),
    )
    out_specs = (P("au", "vert", "ch"), P("ch", "au", "vert"))
    return jax.shard_map(
        per_device, mesh=mesh, in_specs=in_specs, out_specs=out_specs, check_vma=False
    )
```

```python
import jax
import jax.numpy as jnp
from jax import lax
from jax.experimental import pallas as pl
from jax.experimental.pallas import tpu as pltpu
from jax.sharding import PartitionSpec as P

MESH = pl.DeviceIdType.MESH
F32 = jnp.float32
BF16 = jnp.bfloat16
I32 = jnp.int32

CHAN = 128
OVS = 8
SIGMA = 1.5
TU = 32
TV = 128
EU = TU + 8
EV = TV + 8
TILES = 128
CAP = 32
ROWS = 1024
COLS = 128
STEPS = 128
GROUP = 8
GROUPS = STEPS // GROUP
DEPTH = GROUP * CAP
UB = 4


def mod(value, by):
    return lax.rem(value + by, by)


def nt(lhs, rhs):
    return lax.dot_general(lhs, rhs, (((1,), (1,)), ((), ())), preferred_element_type=F32)


def nn(lhs, rhs):
    return jnp.dot(lhs, rhs, preferred_element_type=F32)


def flag(mask):
    return jnp.where(mask, 1.0, 0.0)


def kernel(
    vis_hbm, tile_hbm, row_hbm, col_hbm, sub_hbm, weight_hbm,
    grid_hbm, cont_hbm,
    vis_ref, tile_ref, cell_row_ref, cell_col_ref, sub_ref, weight_ref, grid_ref, cont_ref,
    col_acc, row_acc, send_v, recv_v, send_m, recv_m, sid_ref, wr_ref, wc_ref,
    row_out, row_in, col_out, col_in, cor_out, cor_in,
    sums, sum_row_in, sum_col_in, sum_cor_in, twin_out, twin_in,
    load_sem, store_sem, send_sem, recv_sem, hsend_sem, hrecv_sem, ssend_sem, srecv_sem, twin_sem, stack_sem,
):
    au, vert, ch = lax.axis_index("au"), lax.axis_index("vert"), lax.axis_index("ch")
    z, xl = lax.rem(vert, 8), vert // 8
    y, core = au // 2, lax.rem(au, 2)

    def target(group, dz):
        dx, dc, dy = lax.rem(group, 2), lax.rem(group // 2, 2), group // 4
        to_au = mod(y + dy, 4) * 2 + mod(core + dc, 2)
        to_vert = mod(xl + dx, 2) * 8 + mod(z + dz, 8)
        return to_au, to_vert

    loads = [
        pltpu.make_async_copy(src, dst, load_sem.at[i])
        for i, (src, dst) in enumerate([
            (tile_hbm, tile_ref), (row_hbm, cell_row_ref), (col_hbm, cell_col_ref),
            (sub_hbm, sub_ref), (weight_hbm, weight_ref), (vis_hbm, vis_ref),
        ])
    ]
    for load in loads:
        load.start()
    barrier = pltpu.get_barrier_semaphore()

    def greet(to_au, to_vert, to_ch, sem):
        pl.semaphore_signal(sem, inc=1, device_id=(to_au, to_vert, to_ch), device_id_type=MESH)

    def greet_stack(sem):
        for group in range(2, GROUPS, 2):
            greet(*target(group, 0), ch, sem)

    for step in range(1, 2 * GROUP):
        greet(*target(step // GROUP, step % GROUP), ch, barrier)
    greet_stack(barrier)
    greet(au, vert, 1 - ch, barrier)
    for load in loads:
        load.wait()

    tile_row = tile_ref[...]
    strict = flag(
        lax.broadcasted_iota(I32, (128, 128), 0) < lax.broadcasted_iota(I32, (128, 128), 1)
    ).astype(BF16)
    sub_iota = lax.broadcasted_iota(I32, (128, 128), 0)
    lane_iota = lax.broadcasted_iota(I32, (128, 128), 1)
    ones = jnp.ones((128, 128), BF16)
    before = jnp.zeros((TILES, 128), F32)
    for part in range(ROWS // 128):
        cut = slice(part * 128, part * 128 + 128)
        hit = flag(sub_iota == tile_row[:, cut])
        hit_low = hit.astype(BF16)
        rank = nn(hit_low, strict) + before
        before = before + nn(hit_low, ones)
        place = jnp.sum(hit * rank, axis=0, keepdims=True).astype(I32)
        sid_ref[:, cut] = tile_row[:, cut] * CAP + place

    spread = flag(
        lax.broadcasted_iota(I32, (COLS // 2, COLS), 0) == lax.broadcasted_iota(I32, (COLS // 2, COLS), 1) // 2
    ).astype(BF16)

    def thirds(values):
        pieces = []
        for _ in range(3):
            pieces.append(values.astype(BF16))
            values = values - pieces[-1].astype(F32)
        return pieces

    weight = sum(nn(piece, spread) for piece in thirds(weight_ref[...]))
    line = lax.broadcasted_iota(I32, (16, COLS), 0)
    mine_only = (line & 1) == (lax.broadcasted_iota(I32, (16, COLS), 1) & 1)
    pick = jnp.zeros((16, COLS), F32)
    for i, piece in enumerate(thirds(weight)):
        pick = jnp.where(mine_only & (line // 2 == i), piece.astype(F32), pick)
    both = nt(pick.astype(BF16), vis_ref[...])
    twin_out[...] = (both[0:2] + both[2:4] + both[4:6]).reshape(2, 1, ROWS)
    swap = pltpu.make_async_remote_copy(
        src_ref=twin_out.at[1 - ch], dst_ref=twin_in, send_sem=twin_sem.at[0], recv_sem=twin_sem.at[1],
        device_id=(au, vert, 1 - ch), device_id_type=MESH,
    )

    def copy_of(kind, group, dz):
        to_au, to_vert = target(group, dz)
        tile = to_au * 16 + to_vert
        step = group * GROUP + dz
        device = (to_au, to_vert, ch)
        src, dst = [(send_v, recv_v), (send_m, recv_m)][kind]
        return pltpu.make_async_remote_copy(
            src_ref=src.at[tile], dst_ref=dst.at[step],
            send_sem=send_sem.at[kind], recv_sem=recv_sem.at[kind, group],
            device_id=device, device_id_type=MESH,
        )

    def fill(group):
        to_au, to_vert = target(group, 0)
        base = to_au * 16 + (to_vert // 8) * 8
        slot = lax.broadcasted_iota(I32, (DEPTH, ROWS), 0) + base * CAP
        pick = flag(slot == sid_ref[...]).astype(BF16)
        send_v[pl.ds(base, GROUP)] = nn(pick, vis_ref[...]).astype(BF16).reshape(GROUP, CAP, COLS)

    def start(kind, group, first):
        for dz in range(first, GROUP):
            copy_of(kind, group, dz).start()

    fill(0)
    pl.semaphore_wait(barrier, 23)
    greet_stack(stack_sem)
    start(0, 0, 1)
    swap.start()
    fill(1)
    start(0, 1, 0)
    mine = au * 16 + vert
    recv_v[0] = send_v[mine]
    fill(2)
    fill(3)
    pl.semaphore_wait(stack_sem, 7)
    start(0, 2, 0)
    start(0, 3, 0)

    low = (sub_ref[0:1, :] * OVS + sub_ref[1:2, :]).astype(F32)
    middle = cell_col_ref[...].astype(F32)
    high = cell_row_ref[...].astype(F32)
    swap.wait()
    fields = [high, middle, low]
    fields += [piece.astype(F32) for piece in thirds(twin_out[ch] + twin_in[...])]
    slots = jnp.zeros((len(fields) * TILES, 128), F32)
    for part in range(ROWS // 128):
        cut = slice(part * 128, part * 128 + 128)
        hit = flag(sub_iota == tile_row[:, cut])
        lane_hit = flag((sub_iota & (CAP - 1)) == (sid_ref[:, cut] & (CAP - 1))).astype(BF16)
        slots += nt(jnp.concatenate([hit * field[:, cut] for field in fields], axis=0).astype(BF16), lane_hit)
    slots = [slots[i * TILES : i * TILES + TILES] for i in range(len(fields))]
    meta = slots[0] * 8192.0 + slots[1] * 64.0 + slots[2]
    quarter = lane_iota // CAP
    turn = lax.rem(sub_iota - z + 8, 4)
    meta = jnp.where(quarter == turn, meta, 0.0)
    meta = jnp.where(quarter == ((turn + 1) & 3), slots[3] + slots[4] + slots[5], meta)
    send_m[...] = meta.reshape(TILES, 1, 128)
    recv_m[0] = send_m[mine]
    for group in range(4):
        start(1, group, 1 if group == 0 else 0)
    grid_ref[...] = jnp.zeros_like(grid_ref)
    col_acc[...] = jnp.zeros_like(col_acc)
    row_acc[...] = jnp.zeros_like(row_acc)
    sums[...] = jnp.zeros_like(sums)

    def fill_step(group, carry):
        fill(group)
        start(0, group, 0)
        start(1, group, 0)
        return carry
    lax.fori_loop(4, GROUPS, fill_step, 0)

    def weights(meta_line):
        m = meta_line.astype(I32)
        a, b, o, p = m >> 13, (m >> 6) & 127, (m >> 3) & 7, m & 7

        def taper(index, extent, inner, cell, offset):
            cell_at = jnp.where(index < inner + 4, index, index - extent) - cell
            x = cell_at.astype(F32) - offset.astype(F32) / OVS
            tap = cell_at + 3
            return jnp.where((tap >= 0) & (tap < 8), jnp.exp(-x * x / (2.0 * SIGMA * SIGMA)), 0.0)

        depth = m.shape[1]
        wr_ref[:, 0:depth] = taper(lax.broadcasted_iota(I32, (EU, depth), 0), EU, TU, a, o)
        wc_ref[:, 0:depth] = taper(lax.broadcasted_iota(I32, (EV, depth), 0), EV, TV, b, p)

    def arrived(group, first, count):
        span = pl.ds(group * GROUP + first, count)
        for kind, ref in enumerate([recv_v, recv_m]):
            pltpu.make_async_copy(ref.at[span], ref.at[span], recv_sem.at[kind, group]).wait()

    def add_chunk(group, groups, before_rows, after_rows):
        base = group * GROUP
        depth = groups * DEPTH
        quarter = lax.broadcasted_iota(I32, (4, 128), 1) // CAP == lax.broadcasted_iota(I32, (4, 128), 0)
        metas, totals = [], []
        for i in range(2 * groups):
            lines = recv_m[pl.ds(base + 4 * i, 4)].reshape(4, 128)
            metas.append(jnp.sum(jnp.where(quarter, lines, 0.0), axis=0, keepdims=True))
            lines = pltpu.roll(lines, 128 - CAP, 1)
            totals.append(jnp.sum(jnp.where(quarter, lines, 0.0), axis=0, keepdims=True))
        weights(jnp.concatenate(metas, axis=1))
        left_high, left_low, _ = thirds(wr_ref[:, 0:depth] * jnp.concatenate(totals, axis=1))
        right_high, right_low, _ = thirds(wc_ref[:, 0:depth])
        sums[:, 0:EV] += nt(left_high, right_high) + nt(left_low, right_high) + nt(left_high, right_low)
        before_rows()
        values = recv_v[pl.ds(base, groups * GROUP)].reshape(depth, COLS)
        for u in [*range(TU, EU, UB), *range(0, TU, UB)]:
            if u == 0:
                after_rows()
            col = wc_ref[:, 0:depth]
            taps = jnp.concatenate([col * wr_ref[u + i : u + i + 1, 0:depth] for i in range(UB)], axis=0)
            product = nn(taps.astype(BF16), values).reshape(UB, EV, COLS)
            if u < TU:
                grid_ref[u : u + UB] += product[:, 0:TV]
                col_acc[u : u + UB] += product[:, TV:EV]
            else:
                row_acc[u - TU : u - TU + UB] += product

    arrived(0, 1, GROUP - 1)
    add_chunk(0, 1, lambda: None, lambda: None)

    def chunk_step(pair, carry):
        group = 2 * pair + 1
        arrived(group, 0, GROUP)
        arrived(group + 1, 0, GROUP)
        add_chunk(group, 2, lambda: None, lambda: None)
        return carry
    lax.fori_loop(0, GROUPS // 2 - 1, chunk_step, 0)
    down, up = mod(au + 1, 8), mod(au + 7, 8)
    right, left = mod(vert + 1, 16), mod(vert + 15, 16)

    def halo(src, dst, number, to_au, to_vert):
        return pltpu.make_async_remote_copy(
            src_ref=src, dst_ref=dst, send_sem=hsend_sem.at[number], recv_sem=hrecv_sem.at[number],
            device_id=(to_au, to_vert, ch), device_id_type=MESH,
        )

    row_halos = [
        halo(row_out.at[0], row_in.at[0], 0, down, vert),
        halo(row_out.at[1], row_in.at[1], 1, up, vert),
        halo(cor_out, cor_in.at[0], 2, down, right),
        halo(cor_out, cor_in.at[1], 3, down, left),
        halo(cor_out, cor_in.at[2], 4, up, right),
        halo(cor_out, cor_in.at[3], 5, up, left),
    ]
    col_halos = [
        halo(col_out, col_in.at[0], 6, au, right),
        halo(col_out, col_in.at[1], 7, au, left),
    ]

    def send_rows():
        row_out[...] = row_acc[:, 0:TV].reshape(2, 4 * TV, COLS).astype(BF16)
        cor_out[...] = row_acc[:, TV:EV].reshape(64, COLS).astype(BF16)
        for copy in row_halos:
            copy.start()

    def part(src, dst, number, to_au, to_vert):
        return pltpu.make_async_remote_copy(
            src_ref=src, dst_ref=dst, send_sem=ssend_sem.at[number], recv_sem=srecv_sem.at[number],
            device_id=(to_au, to_vert, ch), device_id_type=MESH,
        )

    row_sums = sums.at[pl.ds(TU, 8), pl.ds(0, TV)]
    col_sums = sums.at[pl.ds(0, TU), pl.ds(TV, TV)]
    cor_sums = sums.at[pl.ds(TU, 8), pl.ds(TV, TV)]
    parts = [
        part(row_sums, sum_row_in.at[0], 0, down, vert),
        part(row_sums, sum_row_in.at[1], 1, up, vert),
        part(col_sums, sum_col_in.at[0], 2, au, right),
        part(col_sums, sum_col_in.at[1], 3, au, left),
        part(cor_sums, sum_cor_in.at[0], 4, down, right),
        part(cor_sums, sum_cor_in.at[1], 5, down, left),
        part(cor_sums, sum_cor_in.at[2], 6, up, right),
        part(cor_sums, sum_cor_in.at[3], 7, up, left),
    ]

    def send_sums():
        for copy in parts:
            copy.start()

    arrived(GROUPS - 1, 0, GROUP)
    add_chunk(GROUPS - 1, 1, send_sums, send_rows)
    col_out[...] = col_acc[...].reshape(TU * 8, COLS).astype(BF16)
    for copy in col_halos:
        copy.start()

    inner_rows = pl.ds(4, TU - 8)
    blocks = [
        (inner_rows, pl.ds(8, TV - 16)),
        (pl.ds(0, 4), pl.ds(0, TV)),
        (pl.ds(TU - 4, 4), pl.ds(0, TV)),
        (inner_rows, pl.ds(0, 8)),
        (inner_rows, pl.ds(TV - 8, 8)),
    ]
    stores = [
        pltpu.make_async_copy(grid_ref.at[block], grid_hbm.at[block], store_sem.at[i])
        for i, block in enumerate(blocks)
    ]
    stores[0].start()

    for kind, ref in enumerate([recv_v, recv_m]):
        span = pl.ds(1, STEPS - 1)
        pltpu.make_async_copy(ref.at[span], ref.at[span], send_sem.at[kind]).wait()
    for copy in parts:
        copy.wait()
    top = lax.broadcasted_iota(I32, (8, TV), 0) < 4
    lane = lax.broadcasted_iota(I32, (TU, TV), 1)

    def sides(from_left, from_right, rows):
        at = lane[0:rows]
        return jnp.where(at < 4, from_left, 0.0) + jnp.where(at >= TV - 4, pltpu.roll(from_right, TV - 8, 1), 0.0)

    total = sums[0:TU, 0:TV] + sides(sum_col_in[0], sum_col_in[1], TU)
    first = sum_row_in[0] + sides(sum_cor_in[0], sum_cor_in[1], 8)
    last = sum_row_in[1] + sides(sum_cor_in[2], sum_cor_in[3], 8)
    cont_ref[...] = total * (1.0 / CHAN)
    cont_ref[0:8] += jnp.where(top, first, 0.0) * (1.0 / CHAN)
    cont_ref[TU - 8 : TU] += jnp.where(top, 0.0, last) * (1.0 / CHAN)
    cont_store = pltpu.make_async_copy(cont_ref, cont_hbm, store_sem.at[5])
    cont_store.start()
    for copy in row_halos + col_halos:
        copy.wait()

    front = lax.broadcasted_iota(I32, (1, 8, COLS), 1) < 4
    grid_ref[0:4, 0:TV] += row_in[0].astype(F32).reshape(4, TV, COLS)
    grid_ref[TU - 4 : TU, 0:TV] += row_in[1].astype(F32).reshape(4, TV, COLS)
    from_left = col_in[0].astype(F32).reshape(TU, 8, COLS)
    from_right = col_in[1].astype(F32).reshape(TU, 8, COLS)
    grid_ref[0:TU, 0:8] += jnp.where(front, from_left, 0.0)
    grid_ref[0:TU, TV - 8 : TV] += jnp.where(front, 0.0, from_right)
    corners = [cor_in[i].astype(F32).reshape(8, 8, COLS) for i in range(4)]
    grid_ref[0:4, 0:8] += jnp.where(front, corners[0][0:4], 0.0)
    grid_ref[0:4, TV - 8 : TV] += jnp.where(front, 0.0, corners[1][0:4])
    grid_ref[TU - 4 : TU, 0:8] += jnp.where(front, corners[2][4:8], 0.0)
    grid_ref[TU - 4 : TU, TV - 8 : TV] += jnp.where(front, 0.0, corners[3][4:8])

    for store in stores[1:]:
        store.start()
    for store in [*stores, cont_store]:
        store.wait()


def handover(grid_in, cont_in, grid_out, cont_out, grid_ref, cont_ref, in_sem, out_sem):
    cuts = [pl.ds(u, 4) for u in range(0, TU, 4)]
    spots = [(grid_in.at[cut], grid_ref.at[cut], grid_out.at[cut]) for cut in cuts]
    spots.append((cont_in, cont_ref, cont_out))
    takes = [pltpu.make_async_copy(src, via, in_sem.at[i]) for i, (src, via, dst) in enumerate(spots)]
    gives = [pltpu.make_async_copy(via, dst, out_sem.at[i]) for i, (src, via, dst) in enumerate(spots)]
    for take in takes:
        take.start()
    for take, give in zip(takes, gives):
        take.wait()
        give.start()
    for give in gives:
        give.wait()


def per_device(visibilities, owner_tile, cell_row, cell_col, subcell, channel_weight):
    anywhere = pl.BlockSpec(memory_space=pl.ANY)
    shapes = (jax.ShapeDtypeStruct((TU, TV, COLS), F32), jax.ShapeDtypeStruct((TU, TV), F32))
    grid, cont = pl.pallas_call(
        kernel,
        out_shape=shapes,
        in_specs=[anywhere] * 6,
        out_specs=(anywhere, anywhere),
        scratch_shapes=[
            pltpu.VMEM((ROWS, COLS), BF16),
            pltpu.VMEM((1, ROWS), I32),
            pltpu.VMEM((1, ROWS), I32),
            pltpu.VMEM((1, ROWS), I32),
            pltpu.VMEM((2, ROWS), I32),
            pltpu.VMEM((1, COLS // 2), F32),
            pltpu.VMEM((TU, TV, COLS), F32),
            pltpu.VMEM((TU, TV), F32),
            pltpu.VMEM((TU, 8, COLS), F32),
            pltpu.VMEM((8, EV, COLS), F32),
            pltpu.VMEM((TILES, CAP, COLS), BF16),
            pltpu.VMEM((STEPS, CAP, COLS), BF16),
            pltpu.VMEM((TILES, 1, 128), F32),
            pltpu.VMEM((STEPS, 1, 128), F32),
            pltpu.VMEM((1, ROWS), I32),
            pltpu.VMEM((EU, 2 * DEPTH), F32),
            pltpu.VMEM((EV, 2 * DEPTH), F32),
            pltpu.VMEM((2, 4 * TV, COLS), BF16),
            pltpu.VMEM((2, 4 * TV, COLS), BF16),
            pltpu.VMEM((TU * 8, COLS), BF16),
            pltpu.VMEM((2, TU * 8, COLS), BF16),
            pltpu.VMEM((64, COLS), BF16),
            pltpu.VMEM((4, 64, COLS), BF16),
            pltpu.VMEM((EU, 2 * TV), F32),
            pltpu.VMEM((2, 8, TV), F32),
            pltpu.VMEM((2, TU, TV), F32),
            pltpu.VMEM((4, 8, TV), F32),
            pltpu.VMEM((2, 1, ROWS), F32),
            pltpu.VMEM((1, ROWS), F32),
            pltpu.SemaphoreType.DMA((6,)),
            pltpu.SemaphoreType.DMA((6,)),
            pltpu.SemaphoreType.DMA((2,)),
            pltpu.SemaphoreType.DMA((2, GROUPS)),
            pltpu.SemaphoreType.DMA((8,)),
            pltpu.SemaphoreType.DMA((8,)),
            pltpu.SemaphoreType.DMA((8,)),
            pltpu.SemaphoreType.DMA((8,)),
            pltpu.SemaphoreType.DMA((2,)),
            pltpu.SemaphoreType.REGULAR,
        ],
        compiler_params=pltpu.CompilerParams(
            collective_id=0, has_side_effects=True, vmem_limit_bytes=62 * 2**20
        ),
        name="gridding",
    )(
        visibilities, owner_tile.reshape(1, ROWS), cell_row.reshape(1, ROWS),
        cell_col.reshape(1, ROWS), subcell, channel_weight.reshape(1, COLS // 2),
    )
    grid, cont = pl.pallas_call(
        handover,
        out_shape=shapes,
        in_specs=[anywhere] * 2,
        out_specs=(anywhere, anywhere),
        scratch_shapes=[
            pltpu.VMEM((TU, TV, COLS), F32),
            pltpu.VMEM((TU, TV), F32),
            pltpu.SemaphoreType.DMA((9,)),
            pltpu.SemaphoreType.DMA((9,)),
        ],
        compiler_params=pltpu.CompilerParams(vmem_limit_bytes=62 * 2**20),
        name="handover",
    )(grid, cont)
    return grid, cont.reshape(1, TU, TV)


def solution(mesh):
    in_specs = (
        P(("au", "vert"), "ch"),
        P(("au", "vert"), None),
        P(("au", "vert")),
        P(("au", "vert")),
        P(None, ("au", "vert")),
        P("ch"),
    )
    out_specs = (P("au", "vert", "ch"), P("ch", "au", "vert"))
    return jax.shard_map(
        per_device, mesh=mesh, in_specs=in_specs, out_specs=out_specs, check_vma=False
    )
```
